128 devices in a mesh: ctx: 32 (over x, y, core), segment: 2 (over z_hi), mp: 2 (over z_lo).
Axes of the slice: x: 4, y: 4, z: 4 (z_hi: 2, z_lo: 2; z = z_hi * 2 + z_lo), core: 2. Of those that a mesh axis runs over, the one named last changes fastest.
Arguments:
- head_inputs: bfloat16 [32768, 4096], P('ctx', ('segment', 'mp')), may hold values from -0.25 to 0.25
- gate_input: bfloat16 [32768, 4096], P('ctx', ('segment', 'mp')), may hold values from -6 to 6
- state_write: bfloat16 [32768, 512], P('ctx', ('segment', 'mp')), may hold values from -6 to 6
- state_read: bfloat16 [32768, 512], P('ctx', ('segment', 'mp')), may hold values from -6 to 6
- log_decay: float32 [32768, 64], P('ctx', ('segment', 'mp')), may hold values from -1.5 to 0
- norm_gain: float32 [4096], P(('segment', 'mp')), may hold values from 0.1 to 1.9
- out_weight: bfloat16 [4096, 4096], P(('segment', 'mp'), 'ctx'), may hold values from -0.09375 to 0.09375
- residual: bfloat16 [32768, 4096], P(('ctx', 'segment', 'mp')), may hold values from -6 to 6
Outputs:
- layer_out: bfloat16 [32768, 4096], P(('ctx', 'segment', 'mp'))
The draws below stay inside these ranges and needn't reach their ends.
All inputs are finite; a program needn't handle non-finite values.
Results may differ from the reference program's by a relative error of at most 0.014.
Values may be sent and summed in bfloat16 or wider, within the bound.
A program may use at most 128 MiB of HBM per device.

```python
import math
import jax
import jax.numpy as jnp
from jax import lax

HEAD_DIM = 64
STATE = 128
GROUP_HEADS = 16
DW = 4096
SPAN = 256
TOK_DEV = 1024
GROUPS = 4
HEADS = 64
CONTEXT_LENGTH = 32768


def head_rates(key, share_fast):
    key_pick, key_fast, key_slow = jax.random.split(key, 3)
    picked = jax.random.uniform(key_pick, (HEADS,)) < share_fast
    fast_rate = jnp.exp(jax.random.uniform(key_fast, (HEADS,), minval=math.log(1.0 / 50.0), maxval=math.log(1.0 / 20.0)))
    slow_rate = jnp.exp(jax.random.uniform(key_slow, (HEADS,), minval=math.log(0.25), maxval=math.log(0.6))) / CONTEXT_LENGTH
    return jnp.where(picked, fast_rate, slow_rate)


def draw_log_decay(key, part):
    forgetting_speeds = head_rates(key, 0.5)
    key = jax.random.fold_in(key, 3)
    key_rough, key_region, key_where, key_depth = jax.random.split(key, 4)
    rough_jitter = jax.random.uniform(key_rough, (CONTEXT_LENGTH, HEADS), minval=0.5, maxval=1.5)
    sections = CONTEXT_LENGTH // TOK_DEV
    region = jnp.exp(jax.random.uniform(key_region, (sections,), minval=math.log(0.6), maxval=math.log(1.5)))
    window_items = jnp.repeat(region, TOK_DEV)
    item_offsets = jax.random.randint(key_where, (2,), 0, CONTEXT_LENGTH)
    layer_indices = jax.random.uniform(key_depth, (2,), minval=0.22, maxval=0.69)
    episode_spans = jnp.zeros((CONTEXT_LENGTH,), jnp.float32).at[item_offsets].add(layer_indices)
    payload_vectors = -(forgetting_speeds[None, :] * rough_jitter * window_items[:, None] + episode_spans[:, None])
    return payload_vectors.astype(jnp.float32)


def draw_head_inputs(key, part):
    forgetting_speeds = head_rates(key, 0.5)
    key = jax.random.fold_in(key, 7)
    key_values = jax.random.fold_in(key, 0)
    scale = jnp.repeat(jnp.sqrt(2.0 * forgetting_speeds / STATE), HEAD_DIM)
    raw = jnp.clip(jax.random.normal(key_values, (CONTEXT_LENGTH, HEADS * HEAD_DIM)), -6.0, 6.0)
    return (raw * scale[None, :]).astype(jnp.bfloat16)


def shard_levels(stream_key, dims, shards, smallest, high):
    factor_of = 1.0
    for dim, parts in shards:
        steps = jax.random.uniform(jax.random.fold_in(jax.random.fold_in(stream_key, 6), dim), (parts,), jnp.float32, smallest / len(shards), high / len(shards))
        factor_of = factor_of * jnp.repeat(jnp.exp(steps), dims[dim] // parts).reshape((-1,) + (1,) * (len(dims) - 1 - dim))
    return factor_of


def gaussian(own_key, shape, spread, most, cuts=(), dtype=jnp.bfloat16):
    factor_of = shard_levels(own_key, shape, cuts, -0.22, 0.18) if cuts else 1.0
    drawn = jax.random.normal(own_key, shape, jnp.float32) * spread * factor_of
    return jnp.minimum(jnp.maximum(drawn, -most), most).astype(dtype)


def setup_inputs(seed: int = 0) -> dict:
    key_of = jax.random.split(jax.random.key(seed), 9)
    return {
        "head_inputs": draw_head_inputs(jax.random.fold_in(key_of[8], 71), 0),
        "gate_input": gaussian(key_of[1], (CONTEXT_LENGTH, HEADS * HEAD_DIM), 1.0, 6.0, ((0, 32), (1, 4))),
        "state_write": gaussian(key_of[2], (CONTEXT_LENGTH, GROUPS * STATE), 1.0, 6.0, ((0, 32), (1, 4))),
        "state_read": gaussian(key_of[3], (CONTEXT_LENGTH, GROUPS * STATE), 1.0, 6.0, ((0, 32), (1, 4))),
        "log_decay": draw_log_decay(jax.random.fold_in(key_of[8], 71), 0),
        "norm_gain": jnp.clip(1.0 + 0.18 * jax.random.normal(key_of[5], (HEADS * HEAD_DIM,), jnp.float32), 0.1, 1.9),
        "out_weight": gaussian(key_of[6], (HEADS * HEAD_DIM, DW), (HEADS * HEAD_DIM) ** -0.5, 0.09375, ((0, 4), (1, 32))),
        "residual": gaussian(key_of[7], (CONTEXT_LENGTH, DW), 1.0, 6.0, ((0, 128),)),
    }


def reference(head_inputs, gate_input, state_write, state_read, log_decay, norm_gain, out_weight, residual):
    tokens = head_inputs.shape[0]
    spans = tokens // SPAN
    features = HEADS * HEAD_DIM
    head_rows = head_inputs.reshape(spans, SPAN, HEADS, HEAD_DIM)
    write_rows = state_write.reshape(spans, SPAN, GROUPS, STATE)
    read_rows = state_read.reshape(spans, SPAN, GROUPS, STATE)
    decay_rows = log_decay.reshape(spans, SPAN, HEADS)
    rows_index = lax.broadcasted_iota(jnp.int32, (SPAN, SPAN), 0)
    cols_index = lax.broadcasted_iota(jnp.int32, (SPAN, SPAN), 1)
    lower_mask = rows_index >= cols_index

    def span_step(carried, pieces):
        block_inputs, block_write, block_read, block_decay = pieces
        cumulative = jnp.cumsum(block_decay, axis=0)
        cum_heads = cumulative.T
        differences = cum_heads[:, :, None] - cum_heads[:, None, :]
        decay_matrix = jnp.exp(jnp.where(lower_mask[None], differences, -jnp.inf))
        scores = jnp.einsum('ign,jgn->gij', block_read.astype(jnp.float32), block_write.astype(jnp.float32))
        scores_heads = jnp.repeat(scores, GROUP_HEADS, axis=0)
        mixing = (decay_matrix * scores_heads).astype(jnp.bfloat16)
        within_block = jnp.einsum('hij,jhp->ihp', mixing.astype(jnp.float32), block_inputs.astype(jnp.float32))
        read_heads = jnp.repeat(block_read, GROUP_HEADS, axis=1).astype(jnp.float32)
        rounded_state = carried.astype(jnp.bfloat16).astype(jnp.float32)
        carried_part = jnp.einsum('ihn,hnp->ihp', read_heads, rounded_state) * jnp.exp(cumulative)[:, :, None]
        final_log = cumulative[-1]
        weights = jnp.exp(final_log[None, :] - cumulative)
        weighted = (block_inputs * weights[:, :, None]).astype(jnp.bfloat16)
        write_heads = jnp.repeat(block_write, GROUP_HEADS, axis=1).astype(jnp.float32)
        fresh_state = jnp.einsum('jhn,jhp->hnp', write_heads, weighted.astype(jnp.float32))
        next_state = jnp.exp(final_log)[:, None, None] * carried + fresh_state
        return (next_state, (within_block + carried_part).reshape(SPAN, features))
    initial = jnp.zeros((HEADS, STATE, HEAD_DIM), jnp.float32)
    _, outputs = lax.scan(span_step, initial, (head_rows, write_rows, read_rows, decay_rows))
    mixed_heads = outputs.reshape(tokens, features)
    gated = mixed_heads * jax.nn.silu(gate_input.astype(jnp.float32))
    grouped = gated.reshape(tokens, GROUPS, GROUP_HEADS * HEAD_DIM)
    factor = lax.rsqrt(lax.optimization_barrier(jnp.mean(grouped * grouped, axis=2, keepdims=True)) + 1e-05)
    normed = ((grouped * factor).reshape(tokens, features) * norm_gain[None, :]).astype(jnp.bfloat16)
    projected = jnp.dot(normed, out_weight, preferred_element_type=jnp.float32)
    return (residual.astype(jnp.float32) + projected).astype(jnp.bfloat16)
```

```python
import jax
import jax.numpy as jnp
from jax import lax
from jax.experimental import pallas as pl
from jax.experimental.pallas import tpu as pltpu
from jax.sharding import PartitionSpec as P

HEAD_DIM = 64
STATE = 128
SPAN = 256
HEADS = 16
FEATS = HEADS * HEAD_DIM
TOKENS = 1024
SPANS = TOKENS // SPAN
HALF = FEATS // 2
MESH = pl.DeviceIdType.MESH
F32, BF16 = jnp.float32, jnp.bfloat16
ALL = slice(None)

PART_X = ((1, 2, 0), 256, 384)
PART_Y = ((2, 0, 1), 640, 384)
PART_Z = ((0, 1, 2), 0, 256)
PARTS = (PART_X, PART_Y, PART_Z)


def place():
    ctx = lax.axis_index("ctx")
    z = lax.axis_index("segment") * 2 + lax.axis_index("mp")
    return lax.div(ctx, 8), lax.rem(lax.div(ctx, 2), 4), z, lax.rem(ctx, 2)


def device(x, y, z, c):
    return {"ctx": (x * 4 + y) * 2 + c, "segment": lax.div(z, 2), "mp": lax.rem(z, 2)}


def around(value, distance):
    return lax.rem(value + distance, 4)


def shifted(pos, axis, distance):
    moved = list(pos)
    moved[axis] = around(moved[axis], distance)
    return device(*moved)


def dot(a, b, contract=((1,), (0,))):
    return lax.dot_general(a, b, (contract, ((), ())), preferred_element_type=F32)


def split3(v):
    hi = v.astype(BF16)
    rest = v - hi.astype(F32)
    mid = rest.astype(BF16)
    return hi, mid, (rest - mid.astype(F32)).astype(BF16)


class RingGather:
    def __init__(self, W, pos, index, axis, first, count, send, recv, sent):
        self.W, self.pos, self.index, self.axis = W, pos, index, axis
        self.first, self.count, self.send, self.recv, self.sent = first, count, send, recv, sent
        me = pos[axis]
        self.me, self.left, self.right, self.far = me, around(me, 3), around(me, 1), around(me, 2)

    def copy(self, who, half, distance, k):
        index = list(self.index)
        index[self.axis] = who
        first, count = self.first, self.count
        if half is not None:
            count = count // 2
            first = first + half * count
        ref = self.W.at[tuple(index) + (pl.ds(first, count), ALL)]
        return pltpu.make_async_remote_copy(
            src_ref=ref, dst_ref=ref, send_sem=self.send(k), recv_sem=self.recv(k),
            device_id=shifted(self.pos, self.axis, distance), device_id_type=MESH,
        )

    def start(self):
        for distance, k in ((1, 0), (3, 1)):
            c = self.copy(self.me, None, distance, k)
            c.start()
            self.sent.append(c)

    def forward(self):
        self.copy(self.left, None, 1, 0).wait_recv()
        a = self.copy(self.left, 0, 1, 2)
        a.start()
        self.copy(self.right, None, 3, 1).wait_recv()
        b = self.copy(self.right, 1, 3, 3)
        b.start()
        self.sent.extend([a, b])

    def finish(self):
        self.copy(self.far, 0, 1, 2).wait_recv()
        self.copy(self.far, 1, 3, 3).wait_recv()


def kernel(
    x_ref, gate_ref, b_ref, c_ref, ld_ref, gain_ref, w_ref, res_ref, o_ref,
    W, X, G, B, C, LD, RES, cum_s, cum_t, ecx, within, ent, thr, NB, ACT, ACC,
    sib_out, sib_in, sib_d, row_t, row_d, col_t, col_d, inc_out, inc, part_out, part_in,
    load_sem, s1, r1, s2, r2, s3, r3, sx, rx, sa, ra, sf, rf, sp, rp, out_sem,
):
    pos = place()
    x, y, z, c = pos
    sibling = device(x, y, z, 1 - c)
    sent = []

    loads = []
    for i, (src, dst) in enumerate((
        (ld_ref, LD), (w_ref, W.at[x, y, z]), (x_ref, X), (b_ref, B), (c_ref, C), (gate_ref, G), (res_ref, RES),
    )):
        loads.append(pltpu.make_async_copy(src, dst, load_sem.at[i]))
        loads[-1].start()

    barrier = pltpu.get_barrier_semaphore()
    partners = [sibling] + [shifted(pos, a, d) for a in range(3) for d in (1, 3, 2)]
    for p in partners:
        pl.semaphore_signal(barrier, inc=1, device_id=p, device_id_type=MESH)

    def push(src, dst, send, recv, target):
        cp = pltpu.make_async_remote_copy(
            src_ref=src, dst_ref=dst, send_sem=send, recv_sem=recv, device_id=target, device_id_type=MESH
        )
        cp.start()
        sent.append(cp)

    def arrived(dst, send, recv):
        pltpu.make_async_remote_copy(
            src_ref=dst, dst_ref=dst, send_sem=send, recv_sem=recv, device_id=sibling, device_id_type=MESH
        ).wait_recv()

    def sems(array, *at):
        return lambda k: array.at[(*at, k)]

    ph1, ph2, ph3 = [], [], []
    for q, ((a1, a2, a3), first, count) in enumerate(PARTS):
        ph1.append(RingGather(W, pos, list(pos[:3]), a1, first, count, sems(s1, q), sems(r1, q), sent))
        index = list(pos[:3])
        index[a1] = ALL
        ph2.append(RingGather(W, pos, index, a2, first, count, sems(s2, q), sems(r2, q), sent))
        subs = []
        for j, d in enumerate((0, 3, 1, 2)):
            index = list(pos[:3])
            index[a1] = ALL
            index[a2] = around(pos[a2], d)
            subs.append(RingGather(W, pos, index, a3, first, count, sems(s3, q, j), sems(r3, q, j), sent))
        ph3.append(subs)

    tri_r = lax.broadcasted_iota(jnp.int32, (SPAN, SPAN), 0)
    tri_c = lax.broadcasted_iota(jnp.int32, (SPAN, SPAN), 1)
    lower = tri_r >= tri_c
    tri = jnp.where(lower, 1.0, 0.0).astype(BF16)
    head_of = lax.div(lax.broadcasted_iota(jnp.int32, (2 * HEADS, FEATS), 1), HEAD_DIM)
    head_at = lax.rem(lax.broadcasted_iota(jnp.int32, (2 * HEADS, FEATS), 0), HEADS)
    spread = jnp.where(head_of == head_at, 1.0, 0.0).astype(BF16)

    def expand(v):
        hi = v.astype(BF16)
        lo = (v - hi.astype(F32)).astype(BF16)
        return dot(jnp.concatenate([hi, lo], axis=1), spread)

    loads[0].wait()
    for s in range(SPANS):
        hi, mid, lo = split3(LD[s * SPAN:(s + 1) * SPAN, :])
        cum = dot(tri, hi) + dot(tri, mid) + dot(tri, lo)
        cum_s[s] = cum
        cum_t[s] = cum.T
    loads[1].wait()
    pl.semaphore_wait(barrier, len(partners))
    for g in ph1:
        g.start()

    ent[0] = jnp.zeros((STATE, FEATS), F32)
    thr[0] = jnp.ones((8, FEATS), F32)
    for i in (2, 3):
        loads[i].wait()

    def fresh(s):
        rows = slice(s * SPAN, (s + 1) * SPAN)
        cum = cum_s[s]
        weights = expand(jnp.exp(cum[SPAN - 1:, :] - cum))
        weighted = (X[rows, :].astype(F32) * weights).astype(BF16)
        new = dot(B[rows, :], weighted, ((0,), (0,)))
        ecx[s] = expand(jnp.exp(cum))
        decay = ecx[s, SPAN - 1:, :]
        ent[s + 1] = decay * ent[s] + new
        thr[s + 1] = thr[s] * decay

    fresh(0)
    fresh(1)
    for g in ph1:
        g.forward()
    fresh(2)
    fresh(3)
    for g in ph1:
        g.finish()
    for g in ph2:
        g.start()
    for t in ph3:
        t[0].start()

    mine = pl.ds(pl.multiple_of(c * HALF, HALF), HALF)
    other = pl.ds(pl.multiple_of((1 - c) * HALF, HALF), HALF)

    sib_out[...] = ent[SPANS, :, other].astype(BF16)
    push(sib_out, sib_in, sx.at[0], rx.at[0], sibling)
    push(thr.at[SPANS], sib_d, sx.at[1], rx.at[1], sibling)

    for i in (4,):
        loads[i].wait()

    lane_low = lax.broadcasted_iota(jnp.int32, (128, 128), 1) < HEAD_DIM

    def within_span(s):
        rows = slice(s * SPAN, (s + 1) * SPAN)
        scores = dot(C[rows, :], B[rows, :], ((1,), (1,)))
        scores = jnp.where(lower, scores, 0.0)
        top, bottom = scores[:128, :128], scores[128:, :]
        cum, cum_row = cum_s[s], cum_t[s]
        for pair in range(HEADS // 2):
            lanes = slice(pair * 128, (pair + 1) * 128)
            xs = X[rows, lanes]
            tops, bottoms = [], []
            for h in (2 * pair, 2 * pair + 1):
                col, row = cum[:, h:h + 1], cum_row[h:h + 1, :]
                mix = (jnp.exp(jnp.minimum(col[:128] - row[:, :128], 0.0)) * top).astype(BF16)
                tops.append(dot(mix, xs[:128]))
                mix = (jnp.exp(jnp.minimum(col[128:] - row, 0.0)) * bottom).astype(BF16)
                bottoms.append(dot(mix, xs))
            within[s, :128, lanes] = jnp.where(lane_low, tops[0], tops[1])
            within[s, 128:, lanes] = jnp.where(lane_low, bottoms[0], bottoms[1])

    within_span(0)

    arrived(sib_in, sx.at[0], rx.at[0])
    arrived(sib_d, sx.at[1], rx.at[1])
    first_core = c == 0
    own_state, own_decay = ent[SPANS, :, mine], thr[SPANS, 0:1, mine]
    sib_state, sib_decay = sib_in[...].astype(F32), sib_d[0:1, mine]
    state0 = jnp.where(first_core, own_state, sib_state)
    state1 = jnp.where(first_core, sib_state, own_state)
    decay0 = jnp.where(first_core, own_decay, sib_decay)
    decay1 = jnp.where(first_core, sib_decay, own_decay)

    def exchange(states, decays, axis, state, decay, at):
        me = pos[axis]
        states[me] = state.astype(BF16)
        decays[me] = jnp.broadcast_to(decay, (8, HALF))
        for i, d in enumerate((1, 3, 2)):
            target = shifted(pos, axis, d)
            push(states.at[me], states.at[me], sx.at[at + i], rx.at[at + i], target)
            push(decays.at[me], decays.at[me], sx.at[at + 3 + i], rx.at[at + 3 + i], target)

    def combine(states, decays, axis, at):
        me = pos[axis]
        for i, d in enumerate((3, 1, 2)):
            who = around(me, d)
            arrived(states.at[who], sx.at[at + i], rx.at[at + i])
            arrived(decays.at[who], sx.at[at + 3 + i], rx.at[at + 3 + i])
        before = jnp.zeros((STATE, HALF), F32)
        through = jnp.ones((1, HALF), F32)
        total, total_decay = before, through
        for t in range(4):
            state, decay = states[t].astype(F32), decays[t, 0:1, :]
            before = jnp.where(t < me, decay * before + state, before)
            through = jnp.where(t < me, through * decay, through)
            total = decay * total + state
            total_decay = total_decay * decay
        return before, through, total, total_decay

    exchange(row_t, row_d, 1, decay1 * state0 + state1, decay0 * decay1, 2)
    for g, t in zip(ph2, ph3):
        g.forward()
        t[1].start()
        t[2].start()

    within_span(1)

    before_y, through_y, total, total_decay = combine(row_t, row_d, 1, 2)
    exchange(col_t, col_d, 0, total, total_decay, 8)
    for g, t in zip(ph2, ph3):
        g.finish()
        t[3].start()

    within_span(2)

    before_x, _, _, _ = combine(col_t, col_d, 0, 8)
    enter0 = through_y * before_x + before_y
    enter1 = decay0 * enter0 + state0
    inc[c] = jnp.where(first_core, enter0, enter1).astype(BF16)
    inc_out[...] = jnp.where(first_core, enter1, enter0).astype(BF16)
    push(inc_out, inc.at[c], sx.at[14], rx.at[14], sibling)

    within_span(3)

    for i in (5, 6):
        loads[i].wait()
    arrived(inc.at[1 - c], sx.at[14], rx.at[14])

    def normed(q):
        rows = pl.ds(pl.multiple_of(q * SPAN, SPAN), SPAN)
        incoming = jnp.concatenate([inc[0], inc[1]], axis=1).astype(F32)
        state = (ent[q] + thr[q, 0:1, :] * incoming).astype(BF16)
        mixed = within[q] + dot(C[rows, :], state) * ecx[q]
        g = G[rows, :].astype(F32)
        gated = mixed * (g / (1.0 + jnp.exp(-g)))
        factor = lax.rsqrt(jnp.mean(gated * gated, axis=1, keepdims=True) + 1e-05)
        return (gated * factor * gain_ref[...]).astype(BF16)

    for i in (1, 2, 3):
        q = around(z, i)
        NB[i - 1] = normed(q)
        push(NB.at[i - 1], ACT.at[c, z], sa.at[i - 1], ra.at[i - 1], device(x, y, q, c))
    ACT[c, z] = normed(z)
    push(ACT.at[c, z], ACT.at[c, z], sf.at[0], rf.at[0], sibling)

    for t in ph3:
        t[0].forward()
    ACC[...] = jnp.zeros(ACC.shape, F32)

    for i in (1, 3, 2):
        who = around(z, 4 - i)
        arrived(ACT.at[c, who], sa.at[i - 1], ra.at[i - 1])
        push(ACT.at[c, who], ACT.at[c, who], sf.at[i], rf.at[i], sibling)
    for j in (1, 2, 3):
        for t in ph3:
            t[j].forward()
    for i in range(4):
        arrived(ACT.at[1 - c, around(z, 4 - i)], sf.at[i], rf.at[i])

    def multiply(b0, b1, zs, first, count):
        total = None
        for zz in zs:
            lhs = ACT[:, zz, :, first:first + count].reshape(2 * SPAN, count)
            rhs = jnp.concatenate(
                [W[b0[0], b0[1], zz, first:first + count, :], W[b1[0], b1[1], zz, first:first + count, :]], axis=1
            )
            d = dot(lhs, rhs)
            total = d if total is None else total + d
        ACC[b0[0], b0[1]] += total[:, :128]
        ACC[b1[0], b1[1]] += total[:, 128:]

    def over_x(first_step, steps):
        _, first, count = PART_X

        @pl.loop(0, 2 * steps)
        def _(i):
            xx = around(x, 3 + first_step + lax.div(i, 2))
            yy = lax.rem(i, 2) * 2
            multiply((xx, yy), (xx, yy + 1), range(4), first, count)

    def over_y(first_step, steps):
        _, first, count = PART_Y

        @pl.loop(0, 2 * steps)
        def _(i):
            yy = around(y, 3 + first_step + lax.div(i, 2))
            xx = lax.rem(i, 2) * 2
            multiply((xx, yy), (xx + 1, yy), range(4), first, count)

    def over_z(distances):
        _, first, count = PART_Z

        @pl.loop(0, 8)
        def _(i):
            xx, yy = lax.div(i, 2), lax.rem(i, 2) * 2
            multiply((xx, yy), (xx, yy + 1), [around(z, d) for d in distances], first, count)

    over_x(0, 3)
    over_y(0, 3)
    over_z((3, 0, 1))
    for q, stage in ((0, lambda: over_x(3, 1)), (1, lambda: over_y(3, 1)), (2, lambda: over_z((2,)))):
        for j in range(4):
            ph3[q][j].finish()
        stage()

    for xx in range(4):
        for yy in range(4):
            rows = pl.ds(pl.multiple_of((1 - c) * SPAN, SPAN), SPAN)
            part_out[xx, yy] = ACC[xx, yy, rows, :].astype(BF16)
        push(part_out.at[xx], part_in.at[xx], sp.at[xx], rp.at[xx], sibling)
    outs = []
    for xx in range(4):
        rows = pl.ds(pl.multiple_of(c * SPAN, SPAN), SPAN)
        for yy in range(4):
            lanes = pl.ds(pl.multiple_of((xx * 8 + yy * 2 + c) * 128, 128), 128)
            RES[:, lanes] = (RES[:, lanes].astype(F32) + ACC[xx, yy, rows, :]).astype(BF16)
        arrived(part_in.at[xx], sp.at[xx], rp.at[xx])
        for yy in range(4):
            lanes = pl.ds(pl.multiple_of((xx * 8 + yy * 2 + 1 - c) * 128, 128), 128)
            RES[:, lanes] = (RES[:, lanes].astype(F32) + part_in[xx, yy].astype(F32)).astype(BF16)
        cols = pl.ds(xx * 1024, 1024)
        outs.append(pltpu.make_async_copy(RES.at[:, cols], o_ref.at[:, cols], out_sem.at[xx]))
        outs[-1].start()
    for cp in outs:
        cp.wait()
    for cp in sent:
        cp.wait_send()


def per_device(
    head_inputs, gate_input, state_write, state_read, log_decay, norm_gain, out_weight, residual
):
    any_space = pl.BlockSpec(memory_space=pl.ANY)
    vmem, dma = pltpu.VMEM, pltpu.SemaphoreType.DMA
    return pl.pallas_call(
        kernel,
        out_shape=jax.ShapeDtypeStruct(residual.shape, BF16),
        in_specs=[any_space] * 5 + [pl.BlockSpec(memory_space=pltpu.VMEM)] + [any_space] * 2,
        out_specs=any_space,
        scratch_shapes=[
            vmem((4, 4, 4, 1024, 128), BF16),
            vmem((TOKENS, FEATS), BF16),
            vmem((TOKENS, FEATS), BF16),
            vmem((TOKENS, STATE), BF16),
            vmem((TOKENS, STATE), BF16),
            vmem((TOKENS, HEADS), F32),
            vmem((SPAN, 4096), BF16),
            vmem((SPANS, SPAN, HEADS), F32),
            vmem((SPANS, HEADS, SPAN), F32),
            vmem((SPANS, SPAN, FEATS), F32),
            vmem((SPANS, SPAN, FEATS), F32),
            vmem((SPANS + 1, STATE, FEATS), F32),
            vmem((SPANS + 1, 8, FEATS), F32),
            vmem((3, SPAN, FEATS), BF16),
            vmem((2, 4, SPAN, FEATS), BF16),
            vmem((4, 4, 2 * SPAN, 128), F32),
            vmem((STATE, HALF), BF16),
            vmem((STATE, HALF), BF16),
            vmem((8, FEATS), F32),
            vmem((4, STATE, HALF), BF16),
            vmem((4, 8, HALF), F32),
            vmem((4, STATE, HALF), BF16),
            vmem((4, 8, HALF), F32),
            vmem((STATE, HALF), BF16),
            vmem((2, STATE, HALF), BF16),
            vmem((4, 4, SPAN, 128), BF16),
            vmem((4, 4, SPAN, 128), BF16),
            dma((7,)),
            dma((3, 4)), dma((3, 4)), dma((3, 4)), dma((3, 4)), dma((3, 4, 4)), dma((3, 4, 4)),
            dma((15,)), dma((15,)),
            dma((3,)), dma((3,)),
            dma((4,)), dma((4,)),
            dma((4,)), dma((4,)),
            dma((4,)),
        ],
        compiler_params=pltpu.CompilerParams(
            collective_id=0, has_side_effects=True, vmem_limit_bytes=60 << 20
        ),
        cost_estimate=pl.CostEstimate(flops=11 * 10**9, bytes_accessed=12 << 20, transcendentals=4 << 20),
        name="spanned_mixer",
    )(head_inputs, gate_input, state_write, state_read, log_decay, norm_gain.reshape(1, -1), out_weight, residual)


def solution(mesh):
    placed = (
        P("ctx", ("segment", "mp")),
        P("ctx", ("segment", "mp")),
        P("ctx", ("segment", "mp")),
        P("ctx", ("segment", "mp")),
        P("ctx", ("segment", "mp")),
        P(("segment", "mp")),
        P(("segment", "mp"), "ctx"),
        P(("ctx", "segment", "mp"), None),
    )
    return jax.shard_map(
        per_device,
        mesh=mesh,
        in_specs=placed,
        out_specs=P(("ctx", "segment", "mp"), None),
        check_vma=False,
    )
```

```python
import jax
import jax.numpy as jnp
from jax import lax
from jax.experimental import pallas as pl
from jax.experimental.pallas import tpu as pltpu
from jax.sharding import PartitionSpec as P

HEAD_DIM = 64
STATE = 128
SPAN = 256
HEADS = 16
FEATS = HEADS * HEAD_DIM
TOKENS = 1024
SPANS = TOKENS // SPAN
HALF = FEATS // 2
MESSAGE = STATE + 16
MESH = pl.DeviceIdType.MESH
F32, BF16 = jnp.float32, jnp.bfloat16
ALL = slice(None)

def place():
    ctx = lax.axis_index("ctx")
    z = lax.axis_index("segment") * 2 + lax.axis_index("mp")
    return lax.div(ctx, 8), lax.rem(lax.div(ctx, 2), 4), z, lax.rem(ctx, 2)


def device(x, y, z, c):
    return {"ctx": (x * 4 + y) * 2 + c, "segment": lax.div(z, 2), "mp": lax.rem(z, 2)}


def around(value, distance):
    return lax.rem(value + distance, 4)


def shifted(pos, axis, distance):
    moved = list(pos)
    moved[axis] = around(moved[axis], distance)
    return device(*moved)


def dot(a, b, contract=((1,), (0,))):
    return lax.dot_general(a, b, (contract, ((), ())), preferred_element_type=F32)


def split3(v):
    hi = v.astype(BF16)
    rest = v - hi.astype(F32)
    mid = rest.astype(BF16)
    return hi, mid, (rest - mid.astype(F32)).astype(BF16)


class RingGather:
    def __init__(self, W, pos, index, axis, send, recv, sent):
        self.W, self.pos, self.index, self.axis = W, pos, index, axis
        self.send, self.recv, self.sent = send, recv, sent
        me = pos[axis]
        self.me, self.left, self.right, self.far = me, around(me, 3), around(me, 1), around(me, 2)

    def copy(self, who, half, distance, k):
        index = list(self.index)
        index[self.axis] = who
        first, count = (0, 1024) if half is None else (512 * half, 512)
        ref = self.W.at[tuple(index) + (pl.ds(first, count), ALL)]
        return pltpu.make_async_remote_copy(
            src_ref=ref, dst_ref=ref, send_sem=self.send(k), recv_sem=self.recv(k),
            device_id=shifted(self.pos, self.axis, distance), device_id_type=MESH,
        )

    def start(self):
        for distance, k in ((1, 0), (3, 1)):
            c = self.copy(self.me, None, distance, k)
            c.start()
            self.sent.append(c)

    def forward(self):
        self.copy(self.left, None, 1, 0).wait_recv()
        a = self.copy(self.left, 0, 1, 2)
        a.start()
        self.copy(self.right, None, 3, 1).wait_recv()
        b = self.copy(self.right, 1, 3, 3)
        b.start()
        self.sent.extend([a, b])

    def finish(self):
        self.copy(self.far, 0, 1, 2).wait_recv()
        self.copy(self.far, 1, 3, 3).wait_recv()


def kernel(
    x_ref, gate_ref, b_ref, c_ref, ld_ref, gain_ref, w_ref, kept_ref, got_ref,
    W, X, G, B, C, LD, cum_s, cum_t, ecx, within, ent, thr, NB, ACT, away, keep,
    sib_out, sib_in, row_out, row_in, col, back_out, back_in, inc_out, inc,
    load_sem, s0, r0, s1, r1, s2, r2, sx, rx, sa, ra, sf, rf, sr, rr, sk, rk, out_sem,
):
    pos = place()
    x, y, z, c = pos
    sibling = device(x, y, z, 1 - c)
    sent = []

    loads = []
    for i, (src, dst) in enumerate((
        (ld_ref, LD), (w_ref, W.at[x, y, 0]), (x_ref, X), (b_ref, B), (c_ref, C), (gate_ref, G),
    )):
        loads.append(pltpu.make_async_copy(src, dst, load_sem.at[i]))
        loads[-1].start()

    barrier = pltpu.get_barrier_semaphore()
    even = 1 - lax.rem(z, 2)
    za, zb = around(z, 3 - 2 * even), around(z, 1 + 2 * even)
    zo = around(z, 2)
    partners = [sibling] + [shifted(pos, a, d) for a in range(2) for d in (1, 3, 2)]
    partners += [device(x, y, zz, cc) for zz in (za, zb) for cc in (0, 1)]
    for p in partners:
        pl.semaphore_signal(barrier, inc=1, device_id=p, device_id_type=MESH)

    def push(src, dst, send, recv, target):
        cp = pltpu.make_async_remote_copy(
            src_ref=src, dst_ref=dst, send_sem=send, recv_sem=recv, device_id=target, device_id_type=MESH
        )
        cp.start()
        sent.append(cp)

    def arrived(dst, send, recv):
        pltpu.make_async_remote_copy(
            src_ref=dst, dst_ref=dst, send_sem=send, recv_sem=recv, device_id=sibling, device_id_type=MESH
        ).wait_recv()

    def sems(array, *at):
        return lambda k: array.at[(*at, k)]

    ph1, ph2 = [], []
    for slot, (a1, a2) in enumerate(((1, 0), (0, 1))):
        ph1.append(RingGather(W, pos, [x, y, slot], a1, sems(s1, slot), sems(r1, slot), sent))
        subs = []
        for j, d in enumerate((0, 3, 1, 2)):
            index = [x, y, slot]
            index[a1] = around(pos[a1], d)
            subs.append(RingGather(W, pos, index, a2, sems(s2, slot, j), sems(r2, slot, j), sent))
        ph2.append(subs)

    tri_r = lax.broadcasted_iota(jnp.int32, (SPAN, SPAN), 0)
    tri_c = lax.broadcasted_iota(jnp.int32, (SPAN, SPAN), 1)
    lower = tri_r >= tri_c
    tri = jnp.where(tri_r <= tri_c, 1.0, 0.0).astype(BF16)
    head_of = lax.div(lax.broadcasted_iota(jnp.int32, (2 * HEADS, FEATS), 1), HEAD_DIM)
    head_at = lax.rem(lax.broadcasted_iota(jnp.int32, (2 * HEADS, FEATS), 0), HEADS)
    spread = jnp.where(head_of == head_at, 1.0, 0.0).astype(BF16)

    def expand(v):
        hi = v.astype(BF16)
        lo = (v - hi.astype(F32)).astype(BF16)
        return dot(jnp.concatenate([hi, lo], axis=1), spread)

    loads[0].wait()
    for s in range(SPANS):
        hi, mid, lo = split3(LD[:, s * SPAN:(s + 1) * SPAN])
        cum = dot(hi, tri) + dot(mid, tri) + dot(lo, tri)
        cum_t[s] = cum
        cum_s[s] = cum.T
    loads[1].wait()
    pl.semaphore_wait(barrier, len(partners))
    odd_y = lax.rem(y, 2)
    zp = around(z, (1 - odd_y) * (3 - 2 * even) + odd_y * (1 + 2 * even))
    push(W.at[x, y, 0], W.at[x, y, 1], s0, r0, device(x, y, zp, c))
    ph1[0].start()
    ph2[0][0].start()

    ent[0] = jnp.zeros((STATE, FEATS), F32)
    thr[0] = jnp.ones((8, FEATS), F32)
    for i in (2, 3):
        loads[i].wait()

    def fresh(s):
        rows = slice(s * SPAN, (s + 1) * SPAN)
        cum = cum_s[s]
        weights = expand(jnp.exp(cum[SPAN - 1:, :] - cum))
        weighted = (X[rows, :].astype(F32) * weights).astype(BF16)
        new = dot(B[rows, :], weighted, ((0,), (0,)))
        ecx[s] = expand(jnp.exp(cum))
        decay = ecx[s, SPAN - 1:, :]
        ent[s + 1] = decay * ent[s] + new
        thr[s + 1] = thr[s] * decay

    for s in range(SPANS):
        fresh(s)

    mine = pl.ds(pl.multiple_of(c * HALF, HALF), HALF)
    other = pl.ds(pl.multiple_of((1 - c) * HALF, HALF), HALF)

    def message(state, decay):
        hi = decay.astype(BF16)
        lo = (decay - hi.astype(F32)).astype(BF16)
        shape = (8, decay.shape[1])
        return state.astype(BF16), jnp.concatenate([jnp.broadcast_to(hi, shape), jnp.broadcast_to(lo, shape)], axis=0)

    def opened(block):
        return block[:STATE].astype(F32), block[STATE:STATE + 1].astype(F32) + block[STATE + 8:STATE + 9].astype(F32)

    sib_out[:STATE], sib_out[STATE:] = message(ent[SPANS, :, other], thr[SPANS, 0:1, other])
    push(sib_out, sib_in, sx.at[0], rx.at[0], sibling)

    for i in (4,):
        loads[i].wait()

    lane_low = lax.broadcasted_iota(jnp.int32, (128, 128), 1) < HEAD_DIM

    def within_span(s):
        rows = slice(s * SPAN, (s + 1) * SPAN)
        scores = dot(C[rows, :], B[rows, :], ((1,), (1,)))
        scores = jnp.where(lower, scores, 0.0)
        top, bottom = scores[:128, :128], scores[128:, :]
        cum, cum_row = cum_s[s], cum_t[s]
        for pair in range(HEADS // 2):
            lanes = slice(pair * 128, (pair + 1) * 128)
            xs = X[rows, lanes]
            tops, bottoms = [], []
            for h in (2 * pair, 2 * pair + 1):
                col, row = cum[:, h:h + 1], cum_row[h:h + 1, :]
                mix = (jnp.exp(jnp.minimum(col[:128] - row[:, :128], 0.0)) * top).astype(BF16)
                tops.append(dot(mix, xs[:128]))
                mix = (jnp.exp(jnp.minimum(col[128:] - row, 0.0)) * bottom).astype(BF16)
                bottoms.append(dot(mix, xs))
            within[s, :128, lanes] = jnp.where(lane_low, tops[0], tops[1])
            within[s, 128:, lanes] = jnp.where(lane_low, bottoms[0], bottoms[1])

    arrived(W.at[x, y, 1], s0, r0)
    ph1[1].start()
    ph2[1][0].start()

    arrived(sib_in, sx.at[0], rx.at[0])
    first_core = c == 0
    own_state, own_decay = ent[SPANS, :, mine], thr[SPANS, 0:1, mine]
    sib_state, sib_decay = opened(sib_in[...])
    state0 = jnp.where(first_core, own_state, sib_state)
    state1 = jnp.where(first_core, sib_state, own_state)
    decay0 = jnp.where(first_core, own_decay, sib_decay)
    decay1 = jnp.where(first_core, sib_decay, own_decay)
    chip_state, chip_decay = message(decay1 * state0 + state1, decay0 * decay1)
    for t in range(4):
        row_out[t, :STATE] = chip_state[:, t * 128:(t + 1) * 128]
        row_out[t, STATE:] = chip_decay[:, t * 128:(t + 1) * 128]
    for i in (2, 1, 3):
        to = around(y, i)
        push(row_out.at[to], row_in.at[y], sx.at[i], rx.at[i], shifted(pos, 1, i))
    row_in[y] = row_out[y]

    ph1[0].forward()
    ph2[0][1].start()
    ph2[0][2].start()

    within_span(0)

    for i in (1, 3, 2):
        arrived(row_in.at[around(y, 4 - i)], sx.at[i], rx.at[i])
    before_y, through_y = [jnp.zeros((STATE, 128), F32)], [jnp.ones((1, 128), F32)]
    for t in range(4):
        state, decay = opened(row_in[t])
        before_y.append(decay * before_y[t] + state)
        through_y.append(through_y[t] * decay)
    row_state, row_decay = message(before_y[4], through_y[4])
    col[x, :STATE] = row_state
    col[x, STATE:] = row_decay
    for i in (2, 1, 3):
        push(col.at[x], col.at[x], sx.at[3 + i], rx.at[3 + i], shifted(pos, 0, i))

    ph1[1].forward()
    ph2[1][1].start()
    ph2[1][2].start()
    ph1[0].finish()
    ph2[0][3].start()

    within_span(1)

    for i in (1, 3, 2):
        arrived(col.at[around(x, 4 - i)], sx.at[3 + i], rx.at[3 + i])
    before_x = jnp.zeros((STATE, 128), F32)
    for t in range(4):
        state, decay = opened(col[t])
        before_x = jnp.where(t < x, decay * before_x + state, before_x)
    for t in range(4):
        back_out[t] = (through_y[t] * before_x + before_y[t]).astype(BF16)
    for i in (2, 1, 3):
        to = around(y, i)
        push(back_out.at[to], back_in.at[y], sx.at[6 + i], rx.at[6 + i], shifted(pos, 1, i))
    back_in[y] = back_out[y]

    ph1[1].finish()
    ph2[1][3].start()

    within_span(2)

    for i in (1, 3, 2):
        arrived(back_in.at[around(y, 4 - i)], sx.at[6 + i], rx.at[6 + i])
    enter0 = jnp.concatenate([back_in[t] for t in range(4)], axis=1).astype(F32)
    enter1 = decay0 * enter0 + state0
    inc[c] = jnp.where(first_core, enter0, enter1).astype(BF16)
    inc_out[...] = jnp.where(first_core, enter1, enter0).astype(BF16)
    push(inc_out, inc.at[c], sx.at[10], rx.at[10], sibling)

    for t in ph2:
        t[0].forward()

    within_span(3)

    for i in (5,):
        loads[i].wait()
    arrived(inc.at[1 - c], sx.at[10], rx.at[10])

    def normed(q):
        rows = pl.ds(pl.multiple_of(q * SPAN, SPAN), SPAN)
        incoming = jnp.concatenate([inc[0], inc[1]], axis=1).astype(F32)
        state = (ent[q] + thr[q, 0:1, :] * incoming).astype(BF16)
        mixed = within[q] + dot(C[rows, :], state) * ecx[q]
        g = G[rows, :].astype(F32)
        gated = mixed * (g / (1.0 + jnp.exp(-g)))
        factor = lax.rsqrt(jnp.mean(gated * gated, axis=1, keepdims=True) + 1e-05)
        return (gated * factor * gain_ref[...]).astype(BF16)

    NB[...] = normed(zo)
    push(NB, ACT.at[3, c], sa.at[0], ra.at[0], device(x, y, za, c))
    push(NB, ACT.at[4, c], sa.at[1], ra.at[1], device(x, y, zb, c))
    ACT[1, c] = normed(za)
    push(ACT.at[1, c], ACT.at[5, c], sa.at[2], ra.at[2], device(x, y, za, c))
    ACT[2, c] = normed(zb)
    push(ACT.at[2, c], ACT.at[6, c], sa.at[3], ra.at[3], device(x, y, zb, c))

    def share(slot):
        push(ACT.at[slot, c], ACT.at[slot, c], sf.at[slot], rf.at[slot], sibling)

    share(1)
    share(2)
    ACT[0, c] = normed(z)
    share(0)

    for j in (1, 2, 3):
        for t in ph2:
            t[j].forward()

    for i in (0, 1):
        arrived(ACT.at[3 + i, c], sa.at[i], ra.at[i])
        share(3 + i)
    for slot in (1, 2, 3, 4):
        arrived(ACT.at[slot, 1 - c], sf.at[slot], rf.at[slot])

    def product(own, other, b0, b1):
        lhs = jnp.concatenate([ACT[own].reshape(2 * SPAN, FEATS), ACT[other].reshape(2 * SPAN, FEATS)], axis=1)
        rhs = jnp.concatenate([W[b[0], b[1]].reshape(2 * FEATS, 128) for b in (b0, b1)], axis=1)
        return dot(lhs, rhs).astype(BF16)

    def columns(bx, by, core):
        return pl.ds(pl.multiple_of((bx * 8 + by * 2 + core) * 128, 128), 128)

    def away_copy(bx, by, section):
        odd = lax.rem(by, 2)
        target = around(z, (1 - odd) * (1 + 2 * even) + odd * (3 - 2 * even))
        return pltpu.make_async_remote_copy(
            src_ref=away.at[bx, by, section], dst_ref=got_ref.at[:, columns(bx, by, c)],
            send_sem=sr.at[bx, by, section], recv_sem=rr.at[bx, by, c],
            device_id=device(x, y, target, section), device_id_type=MESH,
        )

    def keep_local(bx, by):
        return pltpu.make_async_copy(keep.at[bx, by, c], kept_ref.at[:, columns(bx, by, c)], out_sem.at[bx, by])

    def keep_remote(bx, by):
        return pltpu.make_async_remote_copy(
            src_ref=keep.at[bx, by, 1 - c], dst_ref=kept_ref.at[:, columns(bx, by, c)],
            send_sem=sk.at[bx, by], recv_sem=rk.at[bx, by], device_id=sibling, device_id_type=MESH,
        )

    near = (((0, 3), (0, 1)), ((3, 3), (3, 1)), ((1, 3), (1, 1)), ((0, 0), (3, 0)))
    rest = (((1, 0), (2, 0)), ((2, 3), (2, 1)), ((0, 2), (1, 2)), ((2, 2), (3, 2)))

    def over_pairs(table, body):
        @pl.loop(0, 4)
        def _(i):
            def pick(b, axis):
                value = table[0][b][axis]
                for k in (1, 2, 3):
                    value = jnp.where(i == k, table[k][b][axis], value)
                return around(pos[axis], value)

            body((pick(0, 0), pick(0, 1)), (pick(1, 0), pick(1, 1)))

    def send_away(b0, b1):
        odd = lax.rem(b0[1], 2)
        result = product(2 - odd, 3 + odd, b0, b1)
        for k, (bx, by) in enumerate((b0, b1)):
            for section in (0, 1):
                away[bx, by, section] = result[section * SPAN:(section + 1) * SPAN, k * 128:(k + 1) * 128]
                away_copy(bx, by, section).start()

    def keep_here(b0, b1):
        odd = lax.rem(b0[1], 2)
        result = product(0, 5 + odd, b0, b1)
        for k, (bx, by) in enumerate((b0, b1)):
            for section in (0, 1):
                keep[bx, by, section] = result[section * SPAN:(section + 1) * SPAN, k * 128:(k + 1) * 128]
            keep_remote(bx, by).start()
            keep_local(bx, by).start()

    over_pairs(near, send_away)
    for t in ph2:
        for j in range(4):
            t[j].finish()
    over_pairs(rest, send_away)
    for i in (2, 3):
        arrived(ACT.at[3 + i, c], sa.at[i], ra.at[i])
        share(3 + i)
    for slot in (0, 5, 6):
        arrived(ACT.at[slot, 1 - c], sf.at[slot], rf.at[slot])
    over_pairs(near, keep_here)
    over_pairs(rest, keep_here)

    @pl.loop(0, 16)
    def _(i):
        bx, by = lax.div(i, 4), lax.rem(i, 4)
        keep_local(bx, by).wait()
        keep_remote(bx, by).wait_send()
        arrived(kept_ref.at[:, columns(bx, by, 1 - c)], sk.at[bx, by], rk.at[bx, by])
        for section in (0, 1):
            away_copy(bx, by, section).wait_send()
        for core in (0, 1):
            arrived(got_ref.at[:, columns(bx, by, core)], sr.at[bx, by, core], rr.at[bx, by, core])

    for cp in sent:
        cp.wait_send()


def per_device(
    head_inputs, gate_input, state_write, state_read, log_decay, norm_gain, out_weight, residual
):
    any_space = pl.BlockSpec(memory_space=pl.ANY)
    vmem, dma = pltpu.VMEM, pltpu.SemaphoreType.DMA
    kept, got = pl.pallas_call(
        kernel,
        out_shape=[jax.ShapeDtypeStruct(residual.shape, BF16)] * 2,
        in_specs=[any_space] * 5 + [pl.BlockSpec(memory_space=pltpu.VMEM)] + [any_space],
        out_specs=[any_space] * 2,
        scratch_shapes=[
            vmem((4, 4, 2, 1024, 128), BF16),
            vmem((TOKENS, FEATS), BF16),
            vmem((TOKENS, FEATS), BF16),
            vmem((TOKENS, STATE), BF16),
            vmem((TOKENS, STATE), BF16),
            vmem((HEADS, TOKENS), F32),
                vmem((SPANS, SPAN, HEADS), F32),
            vmem((SPANS, HEADS, SPAN), F32),
            vmem((SPANS, SPAN, FEATS), F32),
            vmem((SPANS, SPAN, FEATS), F32),
            vmem((SPANS + 1, STATE, FEATS), F32),
            vmem((SPANS + 1, 8, FEATS), F32),
            vmem((SPAN, FEATS), BF16),
            vmem((7, 2, SPAN, FEATS), BF16),
            vmem((4, 4, 2, SPAN, 128), BF16),
            vmem((4, 4, 2, SPAN, 128), BF16),
            vmem((MESSAGE, HALF), BF16),
            vmem((MESSAGE, HALF), BF16),
            vmem((4, MESSAGE, 128), BF16),
            vmem((4, MESSAGE, 128), BF16),
            vmem((4, MESSAGE, 128), BF16),
            vmem((4, STATE, 128), BF16),
            vmem((4, STATE, 128), BF16),
            vmem((STATE, HALF), BF16),
            vmem((2, STATE, HALF), BF16),
            dma((6,)),
            dma, dma, dma((2, 4)), dma((2, 4)), dma((2, 4, 4)), dma((2, 4, 4)),
            dma((11,)), dma((11,)),
            dma((4,)), dma((4,)),
            dma((7,)), dma((7,)),
            dma((4, 4, 2)), dma((4, 4, 2)),
            dma((4, 4)), dma((4, 4)), dma((4, 4)),
        ],
        compiler_params=pltpu.CompilerParams(
            collective_id=0, has_side_effects=True, vmem_limit_bytes=60 << 20
        ),
        cost_estimate=pl.CostEstimate(flops=11 * 10**9, bytes_accessed=12 << 20, transcendentals=4 << 20),
        name="spanned_mixer",
    )(head_inputs, gate_input, state_write, state_read, log_decay.T, norm_gain.reshape(1, -1), out_weight)
    return (residual.astype(F32) + (kept.astype(F32) + got.astype(F32))).astype(BF16)


def solution(mesh):
    placed = (
        P("ctx", ("segment", "mp")),
        P("ctx", ("segment", "mp")),
        P("ctx", ("segment", "mp")),
        P("ctx", ("segment", "mp")),
        P("ctx", ("segment", "mp")),
        P(("segment", "mp")),
        P(("segment", "mp"), "ctx"),
        P(("ctx", "segment", "mp"), None),
    )
    return jax.shard_map(
        per_device,
        mesh=mesh,
        in_specs=placed,
        out_specs=P(("ctx", "segment", "mp"), None),
        check_vma=False,
    )
```

```python
import jax
import jax.numpy as jnp
from jax import lax
from jax.experimental import pallas as pl
from jax.experimental.pallas import tpu as pltpu
from jax.sharding import PartitionSpec as P

HEAD_DIM = 64
STATE = 128
SPAN = 256
HEADS = 16
FEATS = HEADS * HEAD_DIM
TOKENS = 1024
SPANS = TOKENS // SPAN
HALF = FEATS // 2
MESSAGE = STATE + 16
MESH = pl.DeviceIdType.MESH
F32, BF16 = jnp.float32, jnp.bfloat16
ALL = slice(None)

def place():
    ctx = lax.axis_index("ctx")
    z = lax.axis_index("segment") * 2 + lax.axis_index("mp")
    return lax.div(ctx, 8), lax.rem(lax.div(ctx, 2), 4), z, lax.rem(ctx, 2)


def device(x, y, z, c):
    return {"ctx": (x * 4 + y) * 2 + c, "segment": lax.div(z, 2), "mp": lax.rem(z, 2)}


def around(value, distance):
    return lax.rem(value + distance, 4)


def shifted(pos, axis, distance):
    moved = list(pos)
    moved[axis] = around(moved[axis], distance)
    return device(*moved)


def dot(a, b, contract=((1,), (0,))):
    return lax.dot_general(a, b, (contract, ((), ())), preferred_element_type=F32)


def split3(v):
    hi = v.astype(BF16)
    rest = v - hi.astype(F32)
    mid = rest.astype(BF16)
    return hi, mid, (rest - mid.astype(F32)).astype(BF16)


class RingGather:
    def __init__(self, W, pos, index, axis, first, send, recv, sent):
        self.W, self.pos, self.index, self.axis, self.first = W, pos, index, axis, first
        self.send, self.recv, self.sent = send, recv, sent
        me = pos[axis]
        self.me, self.left, self.right, self.far = me, around(me, 3), around(me, 1), around(me, 2)

    def copy(self, who, half, distance, k):
        index = list(self.index)
        index[self.axis] = who
        first, count = (self.first, 512) if half is None else (self.first + 256 * half, 256)
        ref = self.W.at[tuple(index) + (pl.ds(first, count), ALL)]
        return pltpu.make_async_remote_copy(
            src_ref=ref, dst_ref=ref, send_sem=self.send(k), recv_sem=self.recv(k),
            device_id=shifted(self.pos, self.axis, distance), device_id_type=MESH,
        )

    def start(self):
        for distance, k in ((1, 0), (3, 1)):
            c = self.copy(self.me, None, distance, k)
            c.start()
            self.sent.append(c)

    def forward(self):
        self.copy(self.left, None, 1, 0).wait_recv()
        a = self.copy(self.left, 0, 1, 2)
        a.start()
        self.copy(self.right, None, 3, 1).wait_recv()
        b = self.copy(self.right, 1, 3, 3)
        b.start()
        self.sent.extend([a, b])

    def finish(self):
        self.copy(self.far, 0, 1, 2).wait_recv()
        self.copy(self.far, 1, 3, 3).wait_recv()


def kernel(
    x_ref, gate_ref, b_ref, c_ref, ld_ref, gain_ref, w_ref, res_ref, kept_ref, got_ref,
    W, X, G, B, C, LD, RES, cum_s, cum_t, ecx, within, ent, thr, NB, ACT, away, keep, kin,
    sib_out, sib_in, row_out, row_in, col, back_out, back_in, inc_out, inc,
    load_sem, s0, r0, s1, r1, s2, r2, sx, rx, sa, ra, sf, rf, sr, rr, sk, rk, out_sem,
):
    pos = place()
    x, y, z, c = pos
    sibling = device(x, y, z, 1 - c)
    sent = []

    loads = []
    for i, (src, dst) in enumerate((
        (ld_ref, LD), (w_ref, W.at[x, y, 0]), (x_ref, X), (b_ref, B), (c_ref, C), (gate_ref, G), (res_ref, RES),
    )):
        loads.append(pltpu.make_async_copy(src, dst, load_sem.at[i]))
        loads[-1].start()

    barrier = pltpu.get_barrier_semaphore()
    even = 1 - lax.rem(z, 2)
    za, zb = around(z, 3 - 2 * even), around(z, 1 + 2 * even)
    zo = around(z, 2)
    partners = [sibling] + [shifted(pos, a, d) for a in range(2) for d in (1, 3, 2)]
    partners += [device(x, y, zz, cc) for zz in (za, zb) for cc in (0, 1)]
    for p in partners:
        pl.semaphore_signal(barrier, inc=1, device_id=p, device_id_type=MESH)

    def push(src, dst, send, recv, target):
        cp = pltpu.make_async_remote_copy(
            src_ref=src, dst_ref=dst, send_sem=send, recv_sem=recv, device_id=target, device_id_type=MESH
        )
        cp.start()
        sent.append(cp)

    def arrived(dst, send, recv):
        pltpu.make_async_remote_copy(
            src_ref=dst, dst_ref=dst, send_sem=send, recv_sem=recv, device_id=sibling, device_id_type=MESH
        ).wait_recv()

    def sems(array, *at):
        return lambda k: array.at[(*at, k)]

    ph1, ph2 = [], []
    for part in range(4):
        slot, first = part // 2, part % 2 * 512
        a1, a2 = (1, 0) if part % 2 == 0 else (0, 1)
        ph1.append(RingGather(W, pos, [x, y, slot], a1, first, sems(s1, part), sems(r1, part), sent))
        subs = []
        for j, d in enumerate((0, 3, 1, 2)):
            index = [x, y, slot]
            index[a1] = around(pos[a1], d)
            subs.append(RingGather(W, pos, index, a2, first, sems(s2, part, j), sems(r2, part, j), sent))
        ph2.append(subs)

    tri_r = lax.broadcasted_iota(jnp.int32, (SPAN, SPAN), 0)
    tri_c = lax.broadcasted_iota(jnp.int32, (SPAN, SPAN), 1)
    lower = tri_r >= tri_c
    tri = jnp.where(tri_r <= tri_c, 1.0, 0.0).astype(BF16)
    head_of = lax.div(lax.broadcasted_iota(jnp.int32, (2 * HEADS, FEATS), 1), HEAD_DIM)
    head_at = lax.rem(lax.broadcasted_iota(jnp.int32, (2 * HEADS, FEATS), 0), HEADS)
    spread = jnp.where(head_of == head_at, 1.0, 0.0).astype(BF16)

    def expand(v):
        hi = v.astype(BF16)
        lo = (v - hi.astype(F32)).astype(BF16)
        return dot(jnp.concatenate([hi, lo], axis=1), spread)

    loads[0].wait()
    for s in range(SPANS):
        hi, mid, lo = split3(LD[:, s * SPAN:(s + 1) * SPAN])
        cum = dot(hi, tri) + dot(mid, tri) + dot(lo, tri)
        cum_t[s] = cum
        cum_s[s] = cum.T
    loads[1].wait()
    pl.semaphore_wait(barrier, len(partners))
    odd_y = lax.rem(y, 2)
    zp = around(z, (1 - odd_y) * (3 - 2 * even) + odd_y * (1 + 2 * even))
    push(W.at[x, y, 0], W.at[x, y, 1], s0, r0, device(x, y, zp, c))
    ph1[0].start()
    ph1[1].start()
    ph2[0][0].start()
    ph2[1][0].start()

    ent[0] = jnp.zeros((STATE, FEATS), F32)
    thr[0] = jnp.ones((8, FEATS), F32)
    for i in (2, 3):
        loads[i].wait()

    def fresh(s):
        rows = slice(s * SPAN, (s + 1) * SPAN)
        cum = cum_s[s]
        weights = expand(jnp.exp(cum[SPAN - 1:, :] - cum))
        weighted = (X[rows, :].astype(F32) * weights).astype(BF16)
        new = dot(B[rows, :], weighted, ((0,), (0,)))
        ecx[s] = expand(jnp.exp(cum))
        decay = ecx[s, SPAN - 1:, :]
        ent[s + 1] = decay * ent[s] + new
        thr[s + 1] = thr[s] * decay

    for s in range(SPANS):
        fresh(s)

    mine = pl.ds(pl.multiple_of(c * HALF, HALF), HALF)
    other = pl.ds(pl.multiple_of((1 - c) * HALF, HALF), HALF)

    def message(state, decay):
        hi = decay.astype(BF16)
        lo = (decay - hi.astype(F32)).astype(BF16)
        shape = (8, decay.shape[1])
        return state.astype(BF16), jnp.concatenate([jnp.broadcast_to(hi, shape), jnp.broadcast_to(lo, shape)], axis=0)

    def opened(block):
        return block[:STATE].astype(F32), block[STATE:STATE + 1].astype(F32) + block[STATE + 8:STATE + 9].astype(F32)

    sib_out[:STATE], sib_out[STATE:] = message(ent[SPANS, :, other], thr[SPANS, 0:1, other])
    push(sib_out, sib_in, sx.at[0], rx.at[0], sibling)

    for i in (4, 5):
        loads[i].wait()

    lane_low = lax.broadcasted_iota(jnp.int32, (128, 128), 1) < HEAD_DIM

    def within_span(s):
        rows = slice(s * SPAN, (s + 1) * SPAN)
        scores = dot(C[rows, :], B[rows, :], ((1,), (1,)))
        scores = jnp.where(lower, scores, 0.0)
        top, bottom = scores[:128, :128], scores[128:, :]
        cum, cum_row = cum_s[s], cum_t[s]
        g = G[rows, :].astype(F32)
        silu = g / (1.0 + jnp.exp(-g))
        ecx[s] = ecx[s] * silu
        for pair in range(HEADS // 2):
            lanes = slice(pair * 128, (pair + 1) * 128)
            xs = X[rows, lanes]
            tops, bottoms = [], []
            for h in (2 * pair, 2 * pair + 1):
                col, row = cum[:, h:h + 1], cum_row[h:h + 1, :]
                mix = (jnp.exp(jnp.minimum(col[:128] - row[:, :128], 0.0)) * top).astype(BF16)
                tops.append(dot(mix, xs[:128]))
                mix = (jnp.exp(jnp.minimum(col[128:] - row, 0.0)) * bottom).astype(BF16)
                bottoms.append(dot(mix, xs))
            within[s, :128, lanes] = jnp.where(lane_low, tops[0], tops[1]) * silu[:128, lanes]
            within[s, 128:, lanes] = jnp.where(lane_low, bottoms[0], bottoms[1]) * silu[128:, lanes]

    arrived(sib_in, sx.at[0], rx.at[0])
    first_core = c == 0
    own_state, own_decay = ent[SPANS, :, mine], thr[SPANS, 0:1, mine]
    sib_state, sib_decay = opened(sib_in[...])
    state0 = jnp.where(first_core, own_state, sib_state)
    state1 = jnp.where(first_core, sib_state, own_state)
    decay0 = jnp.where(first_core, own_decay, sib_decay)
    decay1 = jnp.where(first_core, sib_decay, own_decay)
    chip_state, chip_decay = message(decay1 * state0 + state1, decay0 * decay1)
    for t in range(4):
        row_out[t, :STATE] = chip_state[:, t * 128:(t + 1) * 128]
        row_out[t, STATE:] = chip_decay[:, t * 128:(t + 1) * 128]
    for i in (2, 1, 3):
        to = around(y, i)
        push(row_out.at[to], row_in.at[y], sx.at[i], rx.at[i], shifted(pos, 1, i))
    row_in[y] = row_out[y]
    ph1[1].forward()
    ph1[0].forward()
    ph2[0][1].start()

    within_span(0)

    for i in (1, 3, 2):
        arrived(row_in.at[around(y, 4 - i)], sx.at[i], rx.at[i])
    before_y, through_y = [jnp.zeros((STATE, 128), F32)], [jnp.ones((1, 128), F32)]
    for t in range(4):
        state, decay = opened(row_in[t])
        before_y.append(decay * before_y[t] + state)
        through_y.append(through_y[t] * decay)
    row_state, row_decay = message(before_y[4], through_y[4])
    col[x, :STATE] = row_state
    col[x, STATE:] = row_decay
    for i in (2, 1, 3):
        push(col.at[x], col.at[x], sx.at[3 + i], rx.at[3 + i], shifted(pos, 0, i))

    arrived(W.at[x, y, 1], s0, r0)
    ph1[2].start()
    ph1[3].start()
    ph1[0].finish()
    ph1[1].finish()

    within_span(1)

    for i in (1, 3, 2):
        arrived(col.at[around(x, 4 - i)], sx.at[3 + i], rx.at[3 + i])
    before_x = jnp.zeros((STATE, 128), F32)
    for t in range(4):
        state, decay = opened(col[t])
        before_x = jnp.where(t < x, decay * before_x + state, before_x)
    for t in range(4):
        back_out[t] = (through_y[t] * before_x + before_y[t]).astype(BF16)
    for i in (2, 1, 3):
        to = around(y, i)
        push(back_out.at[to], back_in.at[y], sx.at[6 + i], rx.at[6 + i], shifted(pos, 1, i))
    back_in[y] = back_out[y]

    ph1[3].forward()
    ph1[2].forward()
    for j in (1, 2, 3):
        ph2[1][j].start()
        if j > 1:
            ph2[0][j].start()

    within_span(2)

    for i in (1, 3, 2):
        arrived(back_in.at[around(y, 4 - i)], sx.at[6 + i], rx.at[6 + i])
    enter0 = jnp.concatenate([back_in[t] for t in range(4)], axis=1).astype(F32)
    enter1 = decay0 * enter0 + state0
    inc[c] = jnp.where(first_core, enter0, enter1).astype(BF16)
    inc_out[...] = jnp.where(first_core, enter1, enter0).astype(BF16)
    push(inc_out, inc.at[c], sx.at[10], rx.at[10], sibling)

    ph1[2].finish()
    ph1[3].finish()
    ph2[0][0].forward()
    ph2[1][0].forward()

    within_span(3)

    arrived(inc.at[1 - c], sx.at[10], rx.at[10])

    def normed(q):
        rows = pl.ds(pl.multiple_of(q * SPAN, SPAN), SPAN)
        incoming = jnp.concatenate([inc[0], inc[1]], axis=1).astype(F32)
        state = (ent[q] + thr[q, 0:1, :] * incoming).astype(BF16)
        gated = within[q] + dot(C[rows, :], state) * ecx[q]
        factor = lax.rsqrt(jnp.mean(gated * gated, axis=1, keepdims=True) + 1e-05)
        return (gated * factor * gain_ref[...]).astype(BF16)

    NB[...] = normed(zo)
    push(NB, ACT.at[3, c], sa.at[0], ra.at[0], device(x, y, za, c))
    push(NB, ACT.at[4, c], sa.at[1], ra.at[1], device(x, y, zb, c))
    for j in range(4):
        ph2[2][j].start()
        ph2[3][j].start()
    ACT[1, c] = normed(za)
    push(ACT.at[1, c], ACT.at[5, c], sa.at[2], ra.at[2], device(x, y, za, c))
    ACT[2, c] = normed(zb)
    push(ACT.at[2, c], ACT.at[6, c], sa.at[3], ra.at[3], device(x, y, zb, c))

    def share(slot):
        push(ACT.at[slot, c], ACT.at[slot, c], sf.at[slot], rf.at[slot], sibling)

    share(1)
    share(2)
    ACT[0, c] = normed(z)
    share(0)

    for j in (1, 2, 3):
        ph2[0][j].forward()
        ph2[1][j].forward()

    for i in (0, 1):
        arrived(ACT.at[3 + i, c], sa.at[i], ra.at[i])
        share(3 + i)
    for j in range(4):
        ph2[2][j].forward()
        ph2[3][j].forward()
    for slot in (1, 2, 3, 4):
        arrived(ACT.at[slot, 1 - c], sf.at[slot], rf.at[slot])

    def product(own, other, b0, b1):
        lhs = jnp.concatenate([ACT[own].reshape(2 * SPAN, FEATS), ACT[other].reshape(2 * SPAN, FEATS)], axis=1)
        rhs = jnp.concatenate([W[b[0], b[1]].reshape(2 * FEATS, 128) for b in (b0, b1)], axis=1)
        return dot(lhs, rhs)

    def columns(bx, by, core):
        return pl.ds(pl.multiple_of((bx * 8 + by * 2 + core) * 128, 128), 128)

    def away_copy(bx, by, section):
        odd = lax.rem(by, 2)
        target = around(z, (1 - odd) * (1 + 2 * even) + odd * (3 - 2 * even))
        return pltpu.make_async_remote_copy(
            src_ref=away.at[bx, by, section], dst_ref=got_ref.at[:, columns(bx, by, c)],
            send_sem=sr.at[bx, by, section], recv_sem=rr.at[bx, by, c],
            device_id=device(x, y, target, section), device_id_type=MESH,
        )

    def keep_remote(bx, by):
        return pltpu.make_async_remote_copy(
            src_ref=keep.at[bx, by], dst_ref=kin.at[bx, by],
            send_sem=sk.at[bx, by], recv_sem=rk.at[bx, by], device_id=sibling, device_id_type=MESH,
        )

    near = (((0, 3), (0, 1)), ((3, 3), (3, 1)), ((1, 3), (1, 1)), ((0, 0), (3, 0)))
    rest = (((1, 0), (2, 0)), ((2, 3), (2, 1)), ((0, 2), (1, 2)), ((2, 2), (3, 2)))

    def over_pairs(table, body):
        @pl.loop(0, 4)
        def _(i):
            def pick(b, axis):
                value = table[0][b][axis]
                for k in (1, 2, 3):
                    value = jnp.where(i == k, table[k][b][axis], value)
                return around(pos[axis], value)

            body((pick(0, 0), pick(0, 1)), (pick(1, 0), pick(1, 1)))

    def send_away(b0, b1):
        odd = lax.rem(b0[1], 2)
        result = product(2 - odd, 3 + odd, b0, b1)
        for k, (bx, by) in enumerate((b0, b1)):
            for section in (0, 1):
                away[bx, by, section] = result[section * SPAN:(section + 1) * SPAN, k * 128:(k + 1) * 128].astype(BF16)
                away_copy(bx, by, section).start()

    def keep_here(b0, b1):
        odd = lax.rem(b0[1], 2)
        result = product(0, 5 + odd, b0, b1)
        for k, (bx, by) in enumerate((b0, b1)):
            parts = [result[section * SPAN:(section + 1) * SPAN, k * 128:(k + 1) * 128] for section in (0, 1)]
            keep[bx, by] = jnp.where(first_core, parts[1], parts[0]).astype(BF16)
            keep_remote(bx, by).start()
            lanes = columns(bx, by, c)
            RES[:, lanes] = (RES[:, lanes].astype(F32) + jnp.where(first_core, parts[0], parts[1])).astype(BF16)

    over_pairs(near, send_away)
    for i in (2, 3):
        arrived(ACT.at[3 + i, c], sa.at[i], ra.at[i])
        share(3 + i)
    for slot in (0, 5, 6):
        arrived(ACT.at[slot, 1 - c], sf.at[slot], rf.at[slot])
    loads[6].wait()
    over_pairs(near, keep_here)
    for t in ph2:
        for j in range(4):
            t[j].finish()
    over_pairs(rest, send_away)
    over_pairs(rest, keep_here)

    @pl.loop(0, 16)
    def _(i):
        bx, by = lax.div(i, 4), lax.rem(i, 4)
        keep_remote(bx, by).wait_send()
        arrived(kin.at[bx, by], sk.at[bx, by], rk.at[bx, by])
        lanes = columns(bx, by, 1 - c)
        RES[:, lanes] = (RES[:, lanes].astype(F32) + kin[bx, by].astype(F32)).astype(BF16)

    kept_copy = pltpu.make_async_copy(RES, kept_ref, out_sem)
    kept_copy.start()

    for cp in sent:
        cp.wait_send()
    kept_copy.wait()

    @pl.loop(0, 16)
    def _(i):
        bx, by = lax.div(i, 4), lax.rem(i, 4)
        for section in (0, 1):
            away_copy(bx, by, section).wait_send()
        for core in (0, 1):
            arrived(got_ref.at[:, columns(bx, by, core)], sr.at[bx, by, core], rr.at[bx, by, core])


def per_device(
    head_inputs, gate_input, state_write, state_read, log_decay, norm_gain, out_weight, residual
):
    any_space = pl.BlockSpec(memory_space=pl.ANY)
    vmem, dma = pltpu.VMEM, pltpu.SemaphoreType.DMA
    kept, got = pl.pallas_call(
        kernel,
        out_shape=[jax.ShapeDtypeStruct(residual.shape, BF16)] * 2,
        in_specs=[any_space] * 5 + [pl.BlockSpec(memory_space=pltpu.VMEM)] + [any_space] * 2,
        out_specs=[any_space] * 2,
        scratch_shapes=[
            vmem((4, 4, 2, 1024, 128), BF16),
            vmem((TOKENS, FEATS), BF16),
            vmem((TOKENS, FEATS), BF16),
            vmem((TOKENS, STATE), BF16),
            vmem((TOKENS, STATE), BF16),
            vmem((HEADS, TOKENS), F32),
            vmem((SPAN, 4096), BF16),
                vmem((SPANS, SPAN, HEADS), F32),
            vmem((SPANS, HEADS, SPAN), F32),
            vmem((SPANS, SPAN, FEATS), F32),
            vmem((SPANS, SPAN, FEATS), F32),
            vmem((SPANS + 1, STATE, FEATS), F32),
            vmem((SPANS + 1, 8, FEATS), F32),
            vmem((SPAN, FEATS), BF16),
            vmem((7, 2, SPAN, FEATS), BF16),
            vmem((4, 4, 2, SPAN, 128), BF16),
            vmem((4, 4, SPAN, 128), BF16),
            vmem((4, 4, SPAN, 128), BF16),
            vmem((MESSAGE, HALF), BF16),
            vmem((MESSAGE, HALF), BF16),
            vmem((4, MESSAGE, 128), BF16),
            vmem((4, MESSAGE, 128), BF16),
            vmem((4, MESSAGE, 128), BF16),
            vmem((4, STATE, 128), BF16),
            vmem((4, STATE, 128), BF16),
            vmem((STATE, HALF), BF16),
            vmem((2, STATE, HALF), BF16),
            dma((7,)),
            dma, dma, dma((4, 4)), dma((4, 4)), dma((4, 4, 4)), dma((4, 4, 4)),
            dma((11,)), dma((11,)),
            dma((4,)), dma((4,)),
            dma((7,)), dma((7,)),
            dma((4, 4, 2)), dma((4, 4, 2)),
            dma((4, 4)), dma((4, 4)), dma,
        ],
        compiler_params=pltpu.CompilerParams(
            collective_id=0, has_side_effects=True, vmem_limit_bytes=60 << 20
        ),
        cost_estimate=pl.CostEstimate(flops=11 * 10**9, bytes_accessed=12 << 20, transcendentals=4 << 20),
        name="spanned_mixer",
    )(head_inputs, gate_input, state_write, state_read, log_decay.T, norm_gain.reshape(1, -1), out_weight, residual)
    return (kept.astype(F32) + got.astype(F32)).astype(BF16)


def solution(mesh):
    placed = (
        P("ctx", ("segment", "mp")),
        P("ctx", ("segment", "mp")),
        P("ctx", ("segment", "mp")),
        P("ctx", ("segment", "mp")),
        P("ctx", ("segment", "mp")),
        P(("segment", "mp")),
        P(("segment", "mp"), "ctx"),
        P(("ctx", "segment", "mp"), None),
    )
    return jax.shard_map(
        per_device,
        mesh=mesh,
        in_specs=placed,
        out_specs=P(("ctx", "segment", "mp"), None),
        check_vma=False,
    )
```

```python
import jax
import jax.numpy as jnp
from jax import lax
from jax.experimental import pallas as pl
from jax.experimental.pallas import tpu as pltpu
from jax.sharding import PartitionSpec as P

HEAD_DIM = 64
STATE = 128
SPAN = 256
HEADS = 16
FEATS = HEADS * HEAD_DIM
TOKENS = 1024
SPANS = TOKENS // SPAN
HALF = FEATS // 2
MESSAGE = STATE + 16
MESH = pl.DeviceIdType.MESH
F32, BF16 = jnp.float32, jnp.bfloat16
ALL = slice(None)

def place():
    ctx = lax.axis_index("ctx")
    z = lax.axis_index("segment") * 2 + lax.axis_index("mp")
    return lax.div(ctx, 8), lax.rem(lax.div(ctx, 2), 4), z, lax.rem(ctx, 2)


def device(x, y, z, c):
    return {"ctx": (x * 4 + y) * 2 + c, "segment": lax.div(z, 2), "mp": lax.rem(z, 2)}


def around(value, distance):
    return lax.rem(value + distance, 4)


def shifted(pos, axis, distance):
    moved = list(pos)
    moved[axis] = around(moved[axis], distance)
    return device(*moved)


def dot(a, b, contract=((1,), (0,))):
    return lax.dot_general(a, b, (contract, ((), ())), preferred_element_type=F32)


def split3(v):
    hi = v.astype(BF16)
    rest = v - hi.astype(F32)
    mid = rest.astype(BF16)
    return hi, mid, (rest - mid.astype(F32)).astype(BF16)


class RingGather:
    def __init__(self, W, pos, index, axis, first, send, recv, sent):
        self.W, self.pos, self.index, self.axis, self.first = W, pos, index, axis, first
        self.send, self.recv, self.sent = send, recv, sent
        me = pos[axis]
        self.me, self.left, self.right, self.far = me, around(me, 3), around(me, 1), around(me, 2)

    def copy(self, who, half, distance, k):
        index = list(self.index)
        index[self.axis] = who
        first, count = (self.first, 512) if half is None else (self.first + 256 * half, 256)
        ref = self.W.at[tuple(index) + (pl.ds(first, count), ALL)]
        return pltpu.make_async_remote_copy(
            src_ref=ref, dst_ref=ref, send_sem=self.send(k), recv_sem=self.recv(k),
            device_id=shifted(self.pos, self.axis, distance), device_id_type=MESH,
        )

    def start(self):
        for distance, k in ((1, 0), (3, 1)):
            c = self.copy(self.me, None, distance, k)
            c.start()
            self.sent.append(c)

    def forward(self):
        self.copy(self.left, None, 1, 0).wait_recv()
        a = self.copy(self.left, 0, 1, 2)
        a.start()
        self.copy(self.right, None, 3, 1).wait_recv()
        b = self.copy(self.right, 1, 3, 3)
        b.start()
        self.sent.extend([a, b])

    def finish(self):
        self.copy(self.far, 0, 1, 2).wait_recv()
        self.copy(self.far, 1, 3, 3).wait_recv()


def kernel(
    x_ref, gate_ref, b_ref, c_ref, ld_ref, gain_ref, w_ref, res_ref, kept_ref, got_ref,
    W, X, G, B, C, LD, RES, cum_s, cum_t, ecx, within, ent, thr, NB, ACT, away, keep, kin,
    sib_out, sib_in, row_out, row_in, col, back_out, back_in, inc_out, inc,
    load_sem, s0, r0, s1, r1, s2, r2, sx, rx, sa, ra, sf, rf, sr, rr, sk, rk, out_sem,
):
    pos = place()
    x, y, z, c = pos
    sibling = device(x, y, z, 1 - c)
    sent = []

    loads = []
    for i, (src, dst) in enumerate((
        (ld_ref, LD), (w_ref, W.at[x, y, 0]), (x_ref, X), (b_ref, B), (c_ref, C), (gate_ref, G), (res_ref, RES),
    )):
        loads.append(pltpu.make_async_copy(src, dst, load_sem.at[i]))
        loads[-1].start()

    barrier = pltpu.get_barrier_semaphore()
    even = 1 - lax.rem(z, 2)
    za, zb = around(z, 3 - 2 * even), around(z, 1 + 2 * even)
    zo = around(z, 2)
    partners = [sibling] + [shifted(pos, a, d) for a in range(2) for d in (1, 3, 2)]
    partners += [device(x, y, zz, cc) for zz in (za, zb) for cc in (0, 1)]
    for p in partners:
        pl.semaphore_signal(barrier, inc=1, device_id=p, device_id_type=MESH)

    def push(src, dst, send, recv, target):
        cp = pltpu.make_async_remote_copy(
            src_ref=src, dst_ref=dst, send_sem=send, recv_sem=recv, device_id=target, device_id_type=MESH
        )
        cp.start()
        sent.append(cp)

    def arrived(dst, send, recv):
        pltpu.make_async_remote_copy(
            src_ref=dst, dst_ref=dst, send_sem=send, recv_sem=recv, device_id=sibling, device_id_type=MESH
        ).wait_recv()

    def sems(array, *at):
        return lambda k: array.at[(*at, k)]

    ph1, ph2 = [], []
    for part in range(4):
        slot, first = part // 2, part % 2 * 512
        a1, a2 = (1, 0) if part % 2 == 0 else (0, 1)
        ph1.append(RingGather(W, pos, [x, y, slot], a1, first, sems(s1, part), sems(r1, part), sent))
        subs = []
        for j, d in enumerate((0, 3, 1, 2)):
            index = [x, y, slot]
            index[a1] = around(pos[a1], d)
            subs.append(RingGather(W, pos, index, a2, first, sems(s2, part, j), sems(r2, part, j), sent))
        ph2.append(subs)

    tri_r = lax.broadcasted_iota(jnp.int32, (SPAN, SPAN), 0)
    tri_c = lax.broadcasted_iota(jnp.int32, (SPAN, SPAN), 1)
    lower = tri_r >= tri_c
    tri = jnp.where(tri_r <= tri_c, 1.0, 0.0).astype(BF16)
    head_of = lax.div(lax.broadcasted_iota(jnp.int32, (2 * HEADS, FEATS), 1), HEAD_DIM)
    head_at = lax.rem(lax.broadcasted_iota(jnp.int32, (2 * HEADS, FEATS), 0), HEADS)
    spread = jnp.where(head_of == head_at, 1.0, 0.0).astype(BF16)

    def expand(v):
        hi = v.astype(BF16)
        lo = (v - hi.astype(F32)).astype(BF16)
        return dot(jnp.concatenate([hi, lo], axis=1), spread)

    loads[0].wait()
    for s in range(SPANS):
        hi, mid, lo = split3(LD[:, s * SPAN:(s + 1) * SPAN])
        cum = dot(hi, tri) + dot(mid, tri) + dot(lo, tri)
        cum_t[s] = cum
        cum_s[s] = cum.T
    ent[0] = jnp.zeros((STATE, FEATS), F32)
    thr[0] = jnp.ones((8, FEATS), F32)
    for i in (2, 3):
        loads[i].wait()

    def fresh(s):
        rows = slice(s * SPAN, (s + 1) * SPAN)
        cum = cum_s[s]
        weights = expand(jnp.exp(cum[SPAN - 1:, :] - cum))
        weighted = (X[rows, :].astype(F32) * weights).astype(BF16)
        new = dot(B[rows, :], weighted, ((0,), (0,)))
        ecx[s] = expand(jnp.exp(cum))
        decay = ecx[s, SPAN - 1:, :]
        ent[s + 1] = decay * ent[s] + new
        thr[s + 1] = thr[s] * decay

    for s in range(SPANS):
        fresh(s)

    loads[1].wait()
    pl.semaphore_wait(barrier, len(partners))
    odd_y = lax.rem(y, 2)
    zp = around(z, (1 - odd_y) * (3 - 2 * even) + odd_y * (1 + 2 * even))
    push(W.at[x, y, 0], W.at[x, y, 1], s0, r0, device(x, y, zp, c))
    ph1[0].start()
    ph1[1].start()
    ph2[0][0].start()

    mine = pl.ds(pl.multiple_of(c * HALF, HALF), HALF)
    other = pl.ds(pl.multiple_of((1 - c) * HALF, HALF), HALF)

    def message(state, decay):
        hi = decay.astype(BF16)
        lo = (decay - hi.astype(F32)).astype(BF16)
        shape = (8, decay.shape[1])
        return state.astype(BF16), jnp.concatenate([jnp.broadcast_to(hi, shape), jnp.broadcast_to(lo, shape)], axis=0)

    def opened(block):
        return block[:STATE].astype(F32), block[STATE:STATE + 1].astype(F32) + block[STATE + 8:STATE + 9].astype(F32)

    sib_out[:STATE], sib_out[STATE:] = message(ent[SPANS, :, other], thr[SPANS, 0:1, other])
    push(sib_out, sib_in, sx.at[0], rx.at[0], sibling)

    for i in (4, 5):
        loads[i].wait()

    lane_low = lax.broadcasted_iota(jnp.int32, (128, 128), 1) < HEAD_DIM

    def within_span(s):
        rows = slice(s * SPAN, (s + 1) * SPAN)
        scores = dot(C[rows, :], B[rows, :], ((1,), (1,)))
        scores = jnp.where(lower, scores, 0.0)
        top, bottom = scores[:128, :128], scores[128:, :]
        cum, cum_row = cum_s[s], cum_t[s]
        g = G[rows, :].astype(F32)
        silu = g / (1.0 + jnp.exp(-g))
        ecx[s] = ecx[s] * silu
        for pair in range(HEADS // 2):
            lanes = slice(pair * 128, (pair + 1) * 128)
            xs = X[rows, lanes]
            tops, bottoms = [], []
            for h in (2 * pair, 2 * pair + 1):
                col, row = cum[:, h:h + 1], cum_row[h:h + 1, :]
                mix = (jnp.exp(jnp.minimum(col[:128] - row[:, :128], 0.0)) * top).astype(BF16)
                tops.append(dot(mix, xs[:128]))
                mix = (jnp.exp(jnp.minimum(col[128:] - row, 0.0)) * bottom).astype(BF16)
                bottoms.append(dot(mix, xs))
            within[s, :128, lanes] = jnp.where(lane_low, tops[0], tops[1]) * silu[:128, lanes]
            within[s, 128:, lanes] = jnp.where(lane_low, bottoms[0], bottoms[1]) * silu[128:, lanes]

    arrived(sib_in, sx.at[0], rx.at[0])
    first_core = c == 0
    own_state, own_decay = ent[SPANS, :, mine], thr[SPANS, 0:1, mine]
    sib_state, sib_decay = opened(sib_in[...])
    state0 = jnp.where(first_core, own_state, sib_state)
    state1 = jnp.where(first_core, sib_state, own_state)
    decay0 = jnp.where(first_core, own_decay, sib_decay)
    decay1 = jnp.where(first_core, sib_decay, own_decay)
    chip_state, chip_decay = message(decay1 * state0 + state1, decay0 * decay1)
    for t in range(4):
        row_out[t, :STATE] = chip_state[:, t * 128:(t + 1) * 128]
        row_out[t, STATE:] = chip_decay[:, t * 128:(t + 1) * 128]
    for i in (2, 1, 3):
        to = around(y, i)
        push(row_out.at[to], row_in.at[y], sx.at[i], rx.at[i], shifted(pos, 1, i))
    row_in[y] = row_out[y]
    ph1[1].forward()
    ph1[0].forward()

    within_span(0)

    for i in (1, 3, 2):
        arrived(row_in.at[around(y, 4 - i)], sx.at[i], rx.at[i])
    before_y, through_y = [jnp.zeros((STATE, 128), F32)], [jnp.ones((1, 128), F32)]
    for t in range(4):
        state, decay = opened(row_in[t])
        before_y.append(decay * before_y[t] + state)
        through_y.append(through_y[t] * decay)
    row_state, row_decay = message(before_y[4], through_y[4])
    col[x, :STATE] = row_state
    col[x, STATE:] = row_decay
    for i in (2, 1, 3):
        push(col.at[x], col.at[x], sx.at[3 + i], rx.at[3 + i], shifted(pos, 0, i))

    arrived(W.at[x, y, 1], s0, r0)
    ph1[2].start()
    ph1[3].start()
    ph2[1][0].start()
    ph1[0].finish()
    ph2[0][1].start()
    ph1[1].finish()

    within_span(1)

    for i in (1, 3, 2):
        arrived(col.at[around(x, 4 - i)], sx.at[3 + i], rx.at[3 + i])
    before_x = jnp.zeros((STATE, 128), F32)
    for t in range(4):
        state, decay = opened(col[t])
        before_x = jnp.where(t < x, decay * before_x + state, before_x)
    for t in range(4):
        back_out[t] = (through_y[t] * before_x + before_y[t]).astype(BF16)
    for i in (2, 1, 3):
        to = around(y, i)
        push(back_out.at[to], back_in.at[y], sx.at[6 + i], rx.at[6 + i], shifted(pos, 1, i))
    back_in[y] = back_out[y]

    ph1[3].forward()
    ph1[2].forward()
    for j in (1, 2, 3):
        ph2[1][j].start()
        if j > 1:
            ph2[0][j].start()

    within_span(2)

    for i in (1, 3, 2):
        arrived(back_in.at[around(y, 4 - i)], sx.at[6 + i], rx.at[6 + i])
    enter0 = jnp.concatenate([back_in[t] for t in range(4)], axis=1).astype(F32)
    enter1 = decay0 * enter0 + state0
    inc[c] = jnp.where(first_core, enter0, enter1).astype(BF16)
    inc_out[...] = jnp.where(first_core, enter1, enter0).astype(BF16)
    push(inc_out, inc.at[c], sx.at[10], rx.at[10], sibling)

    ph1[2].finish()
    ph1[3].finish()
    ph2[0][0].forward()
    ph2[1][0].forward()

    within_span(3)

    arrived(inc.at[1 - c], sx.at[10], rx.at[10])

    def normed(q, first=0, count=SPAN):
        rows = pl.ds(pl.multiple_of(q * SPAN + first, 128), count)
        incoming = jnp.concatenate([inc[0], inc[1]], axis=1).astype(F32)
        state = (ent[q] + thr[q, 0:1, :] * incoming).astype(BF16)
        here = slice(first, first + count)
        gated = within[q, here] + dot(C[rows, :], state) * ecx[q, here]
        factor = lax.rsqrt(jnp.mean(gated * gated, axis=1, keepdims=True) + 1e-05)
        return (gated * factor * gain_ref[...]).astype(BF16)

    for h in (0, 1):
        half = slice(h * 128, (h + 1) * 128)
        NB[half] = normed(zo, h * 128, 128)
        push(NB.at[half], ACT.at[3, c, half], sa.at[4 * h], ra.at[4 * h], device(x, y, za, c))
        push(NB.at[half], ACT.at[4, c, half], sa.at[4 * h + 1], ra.at[4 * h + 1], device(x, y, zb, c))
    for j in range(4):
        ph2[2][j].start()
        ph2[3][j].start()
    ACT[1, c] = normed(za)
    push(ACT.at[1, c], ACT.at[5, c], sa.at[2], ra.at[2], device(x, y, za, c))
    ACT[2, c] = normed(zb)
    push(ACT.at[2, c], ACT.at[6, c], sa.at[3], ra.at[3], device(x, y, zb, c))

    def share(slot):
        push(ACT.at[slot, c], ACT.at[slot, c], sf.at[slot], rf.at[slot], sibling)

    share(1)
    share(2)
    ACT[0, c] = normed(z)
    share(0)

    for j in (1, 2, 3):
        ph2[0][j].forward()
        ph2[1][j].forward()

    for i in (0, 1):
        for h in (0, 1):
            arrived(ACT.at[3 + i, c, h * 128:(h + 1) * 128], sa.at[4 * h + i], ra.at[4 * h + i])
        share(3 + i)
    for j in range(4):
        ph2[2][j].forward()
        ph2[3][j].forward()
    for slot in (1, 2, 3, 4):
        arrived(ACT.at[slot, 1 - c], sf.at[slot], rf.at[slot])

    def product(own, other, b0, b1):
        lhs = jnp.concatenate([ACT[own].reshape(2 * SPAN, FEATS), ACT[other].reshape(2 * SPAN, FEATS)], axis=1)
        rhs = jnp.concatenate([W[b[0], b[1]].reshape(2 * FEATS, 128) for b in (b0, b1)], axis=1)
        return dot(lhs, rhs)

    def columns(bx, by, core):
        return pl.ds(pl.multiple_of((bx * 8 + by * 2 + core) * 128, 128), 128)

    def away_copy(bx, by, section):
        odd = lax.rem(by, 2)
        target = around(z, (1 - odd) * (1 + 2 * even) + odd * (3 - 2 * even))
        return pltpu.make_async_remote_copy(
            src_ref=away.at[bx, by, section], dst_ref=got_ref.at[:, columns(bx, by, c)],
            send_sem=sr.at[bx, by, section], recv_sem=rr.at[bx, by, c],
            device_id=device(x, y, target, section), device_id_type=MESH,
        )

    def keep_remote(bx, by):
        return pltpu.make_async_remote_copy(
            src_ref=keep.at[bx, by], dst_ref=kin.at[bx, by],
            send_sem=sk.at[bx, by], recv_sem=rk.at[bx, by], device_id=sibling, device_id_type=MESH,
        )

    near = (((0, 3), (0, 1)), ((3, 3), (3, 1)), ((1, 3), (1, 1)), ((0, 0), (3, 0)))
    rest = (((1, 0), (2, 0)), ((2, 3), (2, 1)), ((0, 2), (1, 2)), ((2, 2), (3, 2)))

    def over_pairs(table, body):
        @pl.loop(0, 4)
        def _(i):
            def pick(b, axis):
                value = table[0][b][axis]
                for k in (1, 2, 3):
                    value = jnp.where(i == k, table[k][b][axis], value)
                return around(pos[axis], value)

            body((pick(0, 0), pick(0, 1)), (pick(1, 0), pick(1, 1)))

    def send_away(b0, b1):
        odd = lax.rem(b0[1], 2)
        result = product(2 - odd, 3 + odd, b0, b1)
        for k, (bx, by) in enumerate((b0, b1)):
            for section in (0, 1):
                away[bx, by, section] = result[section * SPAN:(section + 1) * SPAN, k * 128:(k + 1) * 128].astype(BF16)
                away_copy(bx, by, section).start()

    def keep_here(b0, b1):
        odd = lax.rem(b0[1], 2)
        result = product(0, 5 + odd, b0, b1)
        for k, (bx, by) in enumerate((b0, b1)):
            parts = [result[section * SPAN:(section + 1) * SPAN, k * 128:(k + 1) * 128] for section in (0, 1)]
            keep[bx, by] = jnp.where(first_core, parts[1], parts[0]).astype(BF16)
            keep_remote(bx, by).start()
            lanes = columns(bx, by, c)
            RES[:, lanes] = (RES[:, lanes].astype(F32) + jnp.where(first_core, parts[0], parts[1])).astype(BF16)

    over_pairs(near, send_away)
    for i in (2, 3):
        arrived(ACT.at[3 + i, c], sa.at[i], ra.at[i])
        share(3 + i)
    for t in ph2:
        for j in range(4):
            t[j].finish()
    over_pairs(rest, send_away)
    for slot in (0, 5, 6):
        arrived(ACT.at[slot, 1 - c], sf.at[slot], rf.at[slot])
    loads[6].wait()
    over_pairs(near, keep_here)
    over_pairs(rest, keep_here)

    @pl.loop(0, 16)
    def _(i):
        bx, by = lax.div(i, 4), lax.rem(i, 4)
        keep_remote(bx, by).wait_send()
        arrived(kin.at[bx, by], sk.at[bx, by], rk.at[bx, by])
        lanes = columns(bx, by, 1 - c)
        RES[:, lanes] = (RES[:, lanes].astype(F32) + kin[bx, by].astype(F32)).astype(BF16)

    kept_copy = pltpu.make_async_copy(RES, kept_ref, out_sem)
    kept_copy.start()

    for cp in sent:
        cp.wait_send()
    kept_copy.wait()

    @pl.loop(0, 16)
    def _(i):
        bx, by = lax.div(i, 4), lax.rem(i, 4)
        for section in (0, 1):
            away_copy(bx, by, section).wait_send()
        for core in (0, 1):
            arrived(got_ref.at[:, columns(bx, by, core)], sr.at[bx, by, core], rr.at[bx, by, core])


def per_device(
    head_inputs, gate_input, state_write, state_read, log_decay, norm_gain, out_weight, residual
):
    any_space = pl.BlockSpec(memory_space=pl.ANY)
    vmem, dma = pltpu.VMEM, pltpu.SemaphoreType.DMA
    kept, got = pl.pallas_call(
        kernel,
        out_shape=[jax.ShapeDtypeStruct(residual.shape, BF16)] * 2,
        in_specs=[any_space] * 5 + [pl.BlockSpec(memory_space=pltpu.VMEM)] + [any_space] * 2,
        out_specs=[any_space] * 2,
        scratch_shapes=[
            vmem((4, 4, 2, 1024, 128), BF16),
            vmem((TOKENS, FEATS), BF16),
            vmem((TOKENS, FEATS), BF16),
            vmem((TOKENS, STATE), BF16),
            vmem((TOKENS, STATE), BF16),
            vmem((HEADS, TOKENS), F32),
            vmem((SPAN, 4096), BF16),
                vmem((SPANS, SPAN, HEADS), F32),
            vmem((SPANS, HEADS, SPAN), F32),
            vmem((SPANS, SPAN, FEATS), F32),
            vmem((SPANS, SPAN, FEATS), F32),
            vmem((SPANS + 1, STATE, FEATS), F32),
            vmem((SPANS + 1, 8, FEATS), F32),
            vmem((SPAN, FEATS), BF16),
            vmem((7, 2, SPAN, FEATS), BF16),
            vmem((4, 4, 2, SPAN, 128), BF16),
            vmem((4, 4, SPAN, 128), BF16),
            vmem((4, 4, SPAN, 128), BF16),
            vmem((MESSAGE, HALF), BF16),
            vmem((MESSAGE, HALF), BF16),
            vmem((4, MESSAGE, 128), BF16),
            vmem((4, MESSAGE, 128), BF16),
            vmem((4, MESSAGE, 128), BF16),
            vmem((4, STATE, 128), BF16),
            vmem((4, STATE, 128), BF16),
            vmem((STATE, HALF), BF16),
            vmem((2, STATE, HALF), BF16),
            dma((7,)),
            dma, dma, dma((4, 4)), dma((4, 4)), dma((4, 4, 4)), dma((4, 4, 4)),
            dma((11,)), dma((11,)),
            dma((6,)), dma((6,)),
            dma((7,)), dma((7,)),
            dma((4, 4, 2)), dma((4, 4, 2)),
            dma((4, 4)), dma((4, 4)), dma,
        ],
        compiler_params=pltpu.CompilerParams(
            collective_id=0, has_side_effects=True, vmem_limit_bytes=60 << 20
        ),
        cost_estimate=pl.CostEstimate(flops=11 * 10**9, bytes_accessed=12 << 20, transcendentals=4 << 20),
        name="spanned_mixer",
    )(head_inputs, gate_input, state_write, state_read, log_decay.T, norm_gain.reshape(1, -1), out_weight, residual)
    return (kept.astype(F32) + got.astype(F32)).astype(BF16)


def solution(mesh):
    placed = (
        P("ctx", ("segment", "mp")),
        P("ctx", ("segment", "mp")),
        P("ctx", ("segment", "mp")),
        P("ctx", ("segment", "mp")),
        P("ctx", ("segment", "mp")),
        P(("segment", "mp")),
        P(("segment", "mp"), "ctx"),
        P(("ctx", "segment", "mp"), None),
    )
    return jax.shard_map(
        per_device,
        mesh=mesh,
        in_specs=placed,
        out_specs=P(("ctx", "segment", "mp"), None),
        check_vma=False,
    )
```

```python
import jax
import jax.numpy as jnp
from jax import lax
from jax.experimental import pallas as pl
from jax.experimental.pallas import tpu as pltpu
from jax.sharding import PartitionSpec as P

HEAD_DIM = 64
STATE = 128
SPAN = 256
HEADS = 16
FEATS = HEADS * HEAD_DIM
TOKENS = 1024
SPANS = TOKENS // SPAN
HALF = FEATS // 2
MESSAGE = STATE + 16
MESH = pl.DeviceIdType.MESH
F32, BF16 = jnp.float32, jnp.bfloat16
ALL = slice(None)

def place():
    ctx = lax.axis_index("ctx")
    z = lax.axis_index("segment") * 2 + lax.axis_index("mp")
    return lax.div(ctx, 8), lax.rem(lax.div(ctx, 2), 4), z, lax.rem(ctx, 2)


def device(x, y, z, c):
    return {"ctx": (x * 4 + y) * 2 + c, "segment": lax.div(z, 2), "mp": lax.rem(z, 2)}


def around(value, distance):
    return lax.rem(value + distance, 4)


def shifted(pos, axis, distance):
    moved = list(pos)
    moved[axis] = around(moved[axis], distance)
    return device(*moved)


def dot(a, b, contract=((1,), (0,))):
    return lax.dot_general(a, b, (contract, ((), ())), preferred_element_type=F32)


def split3(v):
    hi = v.astype(BF16)
    rest = v - hi.astype(F32)
    mid = rest.astype(BF16)
    return hi, mid, (rest - mid.astype(F32)).astype(BF16)


class RingGather:
    def __init__(self, W, pos, index, axis, first, send, recv, sent):
        self.W, self.pos, self.index, self.axis, self.first = W, pos, index, axis, first
        self.send, self.recv, self.sent = send, recv, sent
        me = pos[axis]
        self.me, self.left, self.right, self.far = me, around(me, 3), around(me, 1), around(me, 2)

    def copy(self, who, half, distance, k):
        index = list(self.index)
        index[self.axis] = who
        first, count = (self.first, 512) if half is None else (self.first + 256 * half, 256)
        ref = self.W.at[tuple(index) + (pl.ds(first, count), ALL)]
        return pltpu.make_async_remote_copy(
            src_ref=ref, dst_ref=ref, send_sem=self.send(k), recv_sem=self.recv(k),
            device_id=shifted(self.pos, self.axis, distance), device_id_type=MESH,
        )

    def start(self):
        for distance, k in ((1, 0), (3, 1)):
            c = self.copy(self.me, None, distance, k)
            c.start()
            self.sent.append(c)

    def forward(self):
        self.copy(self.left, None, 1, 0).wait_recv()
        a = self.copy(self.left, 0, 1, 2)
        a.start()
        self.copy(self.right, None, 3, 1).wait_recv()
        b = self.copy(self.right, 1, 3, 3)
        b.start()
        self.sent.extend([a, b])

    def finish(self):
        self.copy(self.far, 0, 1, 2).wait_recv()
        self.copy(self.far, 1, 3, 3).wait_recv()


def kernel(
    x_ref, gate_ref, b_ref, c_ref, ld_ref, gain_ref, w_ref, res_ref, kept_ref, got_ref,
    W, X, G, B, C, LD, RES, cum_s, cum_t, ecx, within, ent, thr, NB, ACT, away, keep, kin,
    sib_out, sib_in, row_out, row_in, col, back_out, back_in, inc_out, inc,
    load_sem, s0, r0, s1, r1, s2, r2, sx, rx, sa, ra, sf, rf, sr, rr, sk, rk, out_sem,
):
    pos = place()
    x, y, z, c = pos
    sibling = device(x, y, z, 1 - c)
    sent = []

    loads = []
    for i, (src, dst) in enumerate((
        (ld_ref, LD), (w_ref, W.at[x, y, 0]), (x_ref, X), (b_ref, B), (c_ref, C), (gate_ref, G), (res_ref, RES),
    )):
        loads.append(pltpu.make_async_copy(src, dst, load_sem.at[i]))
        loads[-1].start()

    barrier = pltpu.get_barrier_semaphore()
    even = 1 - lax.rem(z, 2)
    za, zb = around(z, 3 - 2 * even), around(z, 1 + 2 * even)
    zo = around(z, 2)
    partners = [sibling] + [shifted(pos, a, d) for a in range(2) for d in (1, 3, 2)]
    partners += [device(x, y, zz, cc) for zz in (za, zb) for cc in (0, 1)]
    for p in partners:
        pl.semaphore_signal(barrier, inc=1, device_id=p, device_id_type=MESH)

    def push(src, dst, send, recv, target):
        cp = pltpu.make_async_remote_copy(
            src_ref=src, dst_ref=dst, send_sem=send, recv_sem=recv, device_id=target, device_id_type=MESH
        )
        cp.start()
        sent.append(cp)

    def arrived(dst, send, recv):
        pltpu.make_async_remote_copy(
            src_ref=dst, dst_ref=dst, send_sem=send, recv_sem=recv, device_id=sibling, device_id_type=MESH
        ).wait_recv()

    def sems(array, *at):
        return lambda k: array.at[(*at, k)]

    ph1, ph2 = [], []
    for part in range(4):
        slot, first = part // 2, part % 2 * 512
        a1, a2 = (1, 0) if part % 2 == 0 else (0, 1)
        ph1.append(RingGather(W, pos, [x, y, slot], a1, first, sems(s1, part), sems(r1, part), sent))
        subs = []
        for j, d in enumerate((0, 3, 1, 2)):
            index = [x, y, slot]
            index[a1] = around(pos[a1], d)
            subs.append(RingGather(W, pos, index, a2, first, sems(s2, part, j), sems(r2, part, j), sent))
        ph2.append(subs)

    tri_r = lax.broadcasted_iota(jnp.int32, (SPAN, SPAN), 0)
    tri_c = lax.broadcasted_iota(jnp.int32, (SPAN, SPAN), 1)
    lower = tri_r >= tri_c
    tri = jnp.where(tri_r <= tri_c, 1.0, 0.0).astype(BF16)
    head_of = lax.div(lax.broadcasted_iota(jnp.int32, (2 * HEADS, FEATS), 1), HEAD_DIM)
    head_at = lax.rem(lax.broadcasted_iota(jnp.int32, (2 * HEADS, FEATS), 0), HEADS)
    spread = jnp.where(head_of == head_at, 1.0, 0.0).astype(BF16)

    def expand(v):
        hi = v.astype(BF16)
        lo = (v - hi.astype(F32)).astype(BF16)
        return dot(jnp.concatenate([hi, lo], axis=1), spread)

    loads[0].wait()
    for s in range(SPANS):
        hi, mid, lo = split3(LD[:, s * SPAN:(s + 1) * SPAN])
        cum = dot(hi, tri) + dot(mid, tri) + dot(lo, tri)
        cum_t[s] = cum
        cum_s[s] = cum.T
    ent[0] = jnp.zeros((STATE, FEATS), F32)
    thr[0] = jnp.ones((8, FEATS), F32)
    for i in (2, 3):
        loads[i].wait()

    def fresh(s):
        rows = slice(s * SPAN, (s + 1) * SPAN)
        cum = cum_s[s]
        weights = expand(jnp.exp(cum[SPAN - 1:, :] - cum))
        weighted = (X[rows, :].astype(F32) * weights).astype(BF16)
        new = dot(B[rows, :], weighted, ((0,), (0,)))
        ecx[s] = expand(jnp.exp(cum))
        decay = ecx[s, SPAN - 1:, :]
        ent[s + 1] = decay * ent[s] + new
        thr[s + 1] = thr[s] * decay

    for s in range(SPANS):
        fresh(s)

    loads[1].wait()
    pl.semaphore_wait(barrier, len(partners))
    odd_y = lax.rem(y, 2)

    def sharer(odd):
        return device(x, y, around(z, (1 - odd) * (3 - 2 * even) + odd * (1 + 2 * even)), c)

    push(W.at[x, y, 0], W.at[x, y, 1], s0, r0, sharer(odd_y))

    def half_block(k, slot):
        d = (3, 1, 2)[k % 3]
        bx, by = (x, around(y, d)) if k < 3 else (around(x, d), y)
        return W.at[bx, by, slot, pl.ds(k // 3 * 512, 512)], lax.rem(by, 2)

    def hand(k):
        src, odd = half_block(k, 0)
        push(src, half_block(k, 1)[0], s1.at[2 + k // 3, k % 3], r1.at[2 + k // 3, k % 3], sharer(odd))

    ph1[0].start()
    ph1[1].start()
    ph2[0][0].start()

    mine = pl.ds(pl.multiple_of(c * HALF, HALF), HALF)
    other = pl.ds(pl.multiple_of((1 - c) * HALF, HALF), HALF)

    def message(state, decay):
        hi = decay.astype(BF16)
        lo = (decay - hi.astype(F32)).astype(BF16)
        shape = (8, decay.shape[1])
        return state.astype(BF16), jnp.concatenate([jnp.broadcast_to(hi, shape), jnp.broadcast_to(lo, shape)], axis=0)

    def opened(block):
        return block[:STATE].astype(F32), block[STATE:STATE + 1].astype(F32) + block[STATE + 8:STATE + 9].astype(F32)

    sib_out[:STATE], sib_out[STATE:] = message(ent[SPANS, :, other], thr[SPANS, 0:1, other])
    push(sib_out, sib_in, sx.at[0], rx.at[0], sibling)

    for i in (4, 5):
        loads[i].wait()

    lane_low = lax.broadcasted_iota(jnp.int32, (128, 128), 1) < HEAD_DIM

    def within_span(s):
        rows = slice(s * SPAN, (s + 1) * SPAN)
        scores = dot(C[rows, :], B[rows, :], ((1,), (1,)))
        scores = jnp.where(lower, scores, 0.0)
        top, bottom = scores[:128, :128], scores[128:, :]
        cum, cum_row = cum_s[s], cum_t[s]
        g = G[rows, :].astype(F32)
        silu = g / (1.0 + jnp.exp(-g))
        ecx[s] = ecx[s] * silu
        for pair in range(HEADS // 2):
            lanes = slice(pair * 128, (pair + 1) * 128)
            xs = X[rows, lanes]
            tops, bottoms = [], []
            for h in (2 * pair, 2 * pair + 1):
                col, row = cum[:, h:h + 1], cum_row[h:h + 1, :]
                mix = (jnp.exp(jnp.minimum(col[:128] - row[:, :128], 0.0)) * top).astype(BF16)
                tops.append(dot(mix, xs[:128]))
                mix = (jnp.exp(jnp.minimum(col[128:] - row, 0.0)) * bottom).astype(BF16)
                bottoms.append(dot(mix, xs))
            within[s, :128, lanes] = jnp.where(lane_low, tops[0], tops[1]) * silu[:128, lanes]
            within[s, 128:, lanes] = jnp.where(lane_low, bottoms[0], bottoms[1]) * silu[128:, lanes]

    arrived(sib_in, sx.at[0], rx.at[0])
    first_core = c == 0
    own_state, own_decay = ent[SPANS, :, mine], thr[SPANS, 0:1, mine]
    sib_state, sib_decay = opened(sib_in[...])
    state0 = jnp.where(first_core, own_state, sib_state)
    state1 = jnp.where(first_core, sib_state, own_state)
    decay0 = jnp.where(first_core, own_decay, sib_decay)
    decay1 = jnp.where(first_core, sib_decay, own_decay)
    chip_state, chip_decay = message(decay1 * state0 + state1, decay0 * decay1)
    for t in range(4):
        row_out[t, :STATE] = chip_state[:, t * 128:(t + 1) * 128]
        row_out[t, STATE:] = chip_decay[:, t * 128:(t + 1) * 128]
    for i in (2, 1, 3):
        to = around(y, i)
        push(row_out.at[to], row_in.at[y], sx.at[i], rx.at[i], shifted(pos, 1, i))
    row_in[y] = row_out[y]
    ph1[1].forward()
    ph1[0].forward()
    for k in (3, 4, 0, 1):
        hand(k)

    within_span(0)

    for i in (1, 3, 2):
        arrived(row_in.at[around(y, 4 - i)], sx.at[i], rx.at[i])
    before_y, through_y = [jnp.zeros((STATE, 128), F32)], [jnp.ones((1, 128), F32)]
    for t in range(4):
        state, decay = opened(row_in[t])
        before_y.append(decay * before_y[t] + state)
        through_y.append(through_y[t] * decay)
    row_state, row_decay = message(before_y[4], through_y[4])
    col[x, :STATE] = row_state
    col[x, STATE:] = row_decay
    for i in (2, 1, 3):
        push(col.at[x], col.at[x], sx.at[3 + i], rx.at[3 + i], shifted(pos, 0, i))

    ph2[1][0].start()
    ph1[0].finish()
    ph2[0][1].start()
    ph1[1].finish()
    for k in (5, 2):
        hand(k)

    within_span(1)

    for i in (1, 3, 2):
        arrived(col.at[around(x, 4 - i)], sx.at[3 + i], rx.at[3 + i])
    before_x = jnp.zeros((STATE, 128), F32)
    for t in range(4):
        state, decay = opened(col[t])
        before_x = jnp.where(t < x, decay * before_x + state, before_x)
    for t in range(4):
        back_out[t] = (through_y[t] * before_x + before_y[t]).astype(BF16)
    for i in (2, 1, 3):
        to = around(y, i)
        push(back_out.at[to], back_in.at[y], sx.at[6 + i], rx.at[6 + i], shifted(pos, 1, i))
    back_in[y] = back_out[y]

    for j in (1, 2, 3):
        ph2[1][j].start()
        if j > 1:
            ph2[0][j].start()

    within_span(2)

    for i in (1, 3, 2):
        arrived(back_in.at[around(y, 4 - i)], sx.at[6 + i], rx.at[6 + i])
    enter0 = jnp.concatenate([back_in[t] for t in range(4)], axis=1).astype(F32)
    enter1 = decay0 * enter0 + state0
    inc[c] = jnp.where(first_core, enter0, enter1).astype(BF16)
    inc_out[...] = jnp.where(first_core, enter1, enter0).astype(BF16)
    push(inc_out, inc.at[c], sx.at[10], rx.at[10], sibling)

    ph2[0][0].forward()
    ph2[1][0].forward()

    within_span(3)

    arrived(inc.at[1 - c], sx.at[10], rx.at[10])

    def normed(q, first=0, count=SPAN):
        rows = pl.ds(pl.multiple_of(q * SPAN + first, 128), count)
        incoming = jnp.concatenate([inc[0], inc[1]], axis=1).astype(F32)
        state = (ent[q] + thr[q, 0:1, :] * incoming).astype(BF16)
        here = slice(first, first + count)
        gated = within[q, here] + dot(C[rows, :], state) * ecx[q, here]
        factor = lax.rsqrt(jnp.mean(gated * gated, axis=1, keepdims=True) + 1e-05)
        return (gated * factor * gain_ref[...]).astype(BF16)

    for h in (0, 1):
        half = slice(h * 128, (h + 1) * 128)
        NB[half] = normed(zo, h * 128, 128)
        push(NB.at[half], ACT.at[3, c, half], sa.at[4 * h], ra.at[4 * h], device(x, y, za, c))
        push(NB.at[half], ACT.at[4, c, half], sa.at[4 * h + 1], ra.at[4 * h + 1], device(x, y, zb, c))
    arrived(W.at[x, y, 1], s0, r0)
    for k in range(6):
        arrived(half_block(k, 1)[0], s1.at[2 + k // 3, k % 3], r1.at[2 + k // 3, k % 3])
    for j in range(4):
        ph2[2][j].start()
        ph2[3][j].start()
    ACT[1, c] = normed(za)
    push(ACT.at[1, c], ACT.at[5, c], sa.at[2], ra.at[2], device(x, y, za, c))
    ACT[2, c] = normed(zb)
    push(ACT.at[2, c], ACT.at[6, c], sa.at[3], ra.at[3], device(x, y, zb, c))

    def share(slot):
        push(ACT.at[slot, c], ACT.at[slot, c], sf.at[slot], rf.at[slot], sibling)

    share(1)
    share(2)
    ACT[0, c] = normed(z)
    share(0)

    for j in (1, 2, 3):
        ph2[0][j].forward()
        ph2[1][j].forward()

    for i in (0, 1):
        for h in (0, 1):
            arrived(ACT.at[3 + i, c, h * 128:(h + 1) * 128], sa.at[4 * h + i], ra.at[4 * h + i])
        share(3 + i)
    for j in range(4):
        ph2[2][j].forward()
        ph2[3][j].forward()
    for slot in (1, 2, 3, 4):
        arrived(ACT.at[slot, 1 - c], sf.at[slot], rf.at[slot])

    def product(own, other, b0, b1):
        lhs = jnp.concatenate([ACT[own].reshape(2 * SPAN, FEATS), ACT[other].reshape(2 * SPAN, FEATS)], axis=1)
        rhs = jnp.concatenate([W[b[0], b[1]].reshape(2 * FEATS, 128) for b in (b0, b1)], axis=1)
        return dot(lhs, rhs)

    def columns(bx, by, core):
        return pl.ds(pl.multiple_of((bx * 8 + by * 2 + core) * 128, 128), 128)

    def away_copy(bx, by, section):
        odd = lax.rem(by, 2)
        target = around(z, (1 - odd) * (1 + 2 * even) + odd * (3 - 2 * even))
        return pltpu.make_async_remote_copy(
            src_ref=away.at[bx, by, section], dst_ref=got_ref.at[:, columns(bx, by, c)],
            send_sem=sr.at[bx, by, section], recv_sem=rr.at[bx, by, c],
            device_id=device(x, y, target, section), device_id_type=MESH,
        )

    def keep_remote(bx, by):
        return pltpu.make_async_remote_copy(
            src_ref=keep.at[bx, by], dst_ref=kin.at[bx, by],
            send_sem=sk.at[bx, by], recv_sem=rk.at[bx, by], device_id=sibling, device_id_type=MESH,
        )

    near = (((0, 3), (0, 1)), ((3, 3), (3, 1)), ((1, 3), (1, 1)), ((0, 0), (3, 0)))
    rest = (((1, 0), (2, 0)), ((2, 3), (2, 1)), ((0, 2), (1, 2)), ((2, 2), (3, 2)))

    def over_pairs(table, body):
        @pl.loop(0, 4)
        def _(i):
            def pick(b, axis):
                value = table[0][b][axis]
                for k in (1, 2, 3):
                    value = jnp.where(i == k, table[k][b][axis], value)
                return around(pos[axis], value)

            body((pick(0, 0), pick(0, 1)), (pick(1, 0), pick(1, 1)))

    def send_away(b0, b1):
        odd = lax.rem(b0[1], 2)
        result = product(2 - odd, 3 + odd, b0, b1)
        for k, (bx, by) in enumerate((b0, b1)):
            for section in (0, 1):
                away[bx, by, section] = result[section * SPAN:(section + 1) * SPAN, k * 128:(k + 1) * 128].astype(BF16)
                away_copy(bx, by, section).start()

    def keep_here(b0, b1):
        odd = lax.rem(b0[1], 2)
        result = product(0, 5 + odd, b0, b1)
        for k, (bx, by) in enumerate((b0, b1)):
            parts = [result[section * SPAN:(section + 1) * SPAN, k * 128:(k + 1) * 128] for section in (0, 1)]
            keep[bx, by] = jnp.where(first_core, parts[1], parts[0]).astype(BF16)
            keep_remote(bx, by).start()
            lanes = columns(bx, by, c)
            RES[:, lanes] = (RES[:, lanes].astype(F32) + jnp.where(first_core, parts[0], parts[1])).astype(BF16)

    over_pairs(near, send_away)
    for i in (2, 3):
        arrived(ACT.at[3 + i, c], sa.at[i], ra.at[i])
        share(3 + i)
    for t in ph2:
        for j in range(4):
            t[j].finish()
    over_pairs(rest, send_away)
    for slot in (0, 5, 6):
        arrived(ACT.at[slot, 1 - c], sf.at[slot], rf.at[slot])
    loads[6].wait()
    over_pairs(near, keep_here)
    over_pairs(rest, keep_here)

    @pl.loop(0, 16)
    def _(i):
        bx, by = lax.div(i, 4), lax.rem(i, 4)
        keep_remote(bx, by).wait_send()
        arrived(kin.at[bx, by], sk.at[bx, by], rk.at[bx, by])
        lanes = columns(bx, by, 1 - c)
        RES[:, lanes] = (RES[:, lanes].astype(F32) + kin[bx, by].astype(F32)).astype(BF16)

    kept_copy = pltpu.make_async_copy(RES, kept_ref, out_sem)
    kept_copy.start()

    for cp in sent:
        cp.wait_send()
    kept_copy.wait()

    @pl.loop(0, 16)
    def _(i):
        bx, by = lax.div(i, 4), lax.rem(i, 4)
        for section in (0, 1):
            away_copy(bx, by, section).wait_send()
        for core in (0, 1):
            arrived(got_ref.at[:, columns(bx, by, core)], sr.at[bx, by, core], rr.at[bx, by, core])


def per_device(
    head_inputs, gate_input, state_write, state_read, log_decay, norm_gain, out_weight, residual
):
    any_space = pl.BlockSpec(memory_space=pl.ANY)
    vmem, dma = pltpu.VMEM, pltpu.SemaphoreType.DMA
    kept, got = pl.pallas_call(
        kernel,
        out_shape=[jax.ShapeDtypeStruct(residual.shape, BF16)] * 2,
        in_specs=[any_space] * 5 + [pl.BlockSpec(memory_space=pltpu.VMEM)] + [any_space] * 2,
        out_specs=[any_space] * 2,
        scratch_shapes=[
            vmem((4, 4, 2, 1024, 128), BF16),
            vmem((TOKENS, FEATS), BF16),
            vmem((TOKENS, FEATS), BF16),
            vmem((TOKENS, STATE), BF16),
            vmem((TOKENS, STATE), BF16),
            vmem((HEADS, TOKENS), F32),
            vmem((SPAN, 4096), BF16),
                vmem((SPANS, SPAN, HEADS), F32),
            vmem((SPANS, HEADS, SPAN), F32),
            vmem((SPANS, SPAN, FEATS), F32),
            vmem((SPANS, SPAN, FEATS), F32),
            vmem((SPANS + 1, STATE, FEATS), F32),
            vmem((SPANS + 1, 8, FEATS), F32),
            vmem((SPAN, FEATS), BF16),
            vmem((7, 2, SPAN, FEATS), BF16),
            vmem((4, 4, 2, SPAN, 128), BF16),
            vmem((4, 4, SPAN, 128), BF16),
            vmem((4, 4, SPAN, 128), BF16),
            vmem((MESSAGE, HALF), BF16),
            vmem((MESSAGE, HALF), BF16),
            vmem((4, MESSAGE, 128), BF16),
            vmem((4, MESSAGE, 128), BF16),
            vmem((4, MESSAGE, 128), BF16),
            vmem((4, STATE, 128), BF16),
            vmem((4, STATE, 128), BF16),
            vmem((STATE, HALF), BF16),
            vmem((2, STATE, HALF), BF16),
            dma((7,)),
            dma, dma, dma((4, 4)), dma((4, 4)), dma((4, 4, 4)), dma((4, 4, 4)),
            dma((11,)), dma((11,)),
            dma((6,)), dma((6,)),
            dma((7,)), dma((7,)),
            dma((4, 4, 2)), dma((4, 4, 2)),
            dma((4, 4)), dma((4, 4)), dma,
        ],
        compiler_params=pltpu.CompilerParams(
            collective_id=0, has_side_effects=True, vmem_limit_bytes=60 << 20
        ),
        cost_estimate=pl.CostEstimate(flops=11 * 10**9, bytes_accessed=12 << 20, transcendentals=4 << 20),
        name="spanned_mixer",
    )(head_inputs, gate_input, state_write, state_read, log_decay.T, norm_gain.reshape(1, -1), out_weight, residual)
    return (kept.astype(F32) + got.astype(F32)).astype(BF16)


def solution(mesh):
    placed = (
        P("ctx", ("segment", "mp")),
        P("ctx", ("segment", "mp")),
        P("ctx", ("segment", "mp")),
        P("ctx", ("segment", "mp")),
        P("ctx", ("segment", "mp")),
        P(("segment", "mp")),
        P(("segment", "mp"), "ctx"),
        P(("ctx", "segment", "mp"), None),
    )
    return jax.shard_map(
        per_device,
        mesh=mesh,
        in_specs=placed,
        out_specs=P(("ctx", "segment", "mp"), None),
        check_vma=False,
    )
```

```python
import jax
import jax.numpy as jnp
from jax import lax
from jax.experimental import pallas as pl
from jax.experimental.pallas import tpu as pltpu
from jax.sharding import PartitionSpec as P

HEAD_DIM = 64
STATE = 128
SPAN = 256
HEADS = 16
FEATS = HEADS * HEAD_DIM
TOKENS = 1024
SPANS = TOKENS // SPAN
HALF = FEATS // 2
MESSAGE = STATE + 16
MESH = pl.DeviceIdType.MESH
F32, BF16 = jnp.float32, jnp.bfloat16
ALL = slice(None)

def place():
    ctx = lax.axis_index("ctx")
    z = lax.axis_index("segment") * 2 + lax.axis_index("mp")
    return lax.div(ctx, 8), lax.rem(lax.div(ctx, 2), 4), z, lax.rem(ctx, 2)


def device(x, y, z, c):
    return {"ctx": (x * 4 + y) * 2 + c, "segment": lax.div(z, 2), "mp": lax.rem(z, 2)}


def around(value, distance):
    return lax.rem(value + distance, 4)


def shifted(pos, axis, distance):
    moved = list(pos)
    moved[axis] = around(moved[axis], distance)
    return device(*moved)


def dot(a, b, contract=((1,), (0,))):
    return lax.dot_general(a, b, (contract, ((), ())), preferred_element_type=F32)


def split3(v):
    hi = v.astype(BF16)
    rest = v - hi.astype(F32)
    mid = rest.astype(BF16)
    return hi, mid, (rest - mid.astype(F32)).astype(BF16)


class RingGather:
    def __init__(self, W, pos, index, axis, first, send, recv, sent):
        self.W, self.pos, self.index, self.axis, self.first = W, pos, index, axis, first
        self.send, self.recv, self.sent = send, recv, sent
        me = pos[axis]
        self.me, self.left, self.right, self.far = me, around(me, 3), around(me, 1), around(me, 2)

    def copy(self, who, half, distance, k):
        index = list(self.index)
        index[self.axis] = who
        first, count = (self.first, 512) if half is None else (self.first + 256 * half, 256)
        ref = self.W.at[tuple(index) + (pl.ds(first, count), ALL)]
        return pltpu.make_async_remote_copy(
            src_ref=ref, dst_ref=ref, send_sem=self.send(k), recv_sem=self.recv(k),
            device_id=shifted(self.pos, self.axis, distance), device_id_type=MESH,
        )

    def start(self):
        for distance, k in ((1, 0), (3, 1)):
            c = self.copy(self.me, None, distance, k)
            c.start()
            self.sent.append(c)

    def forward(self):
        self.copy(self.left, None, 1, 0).wait_recv()
        a = self.copy(self.left, 0, 1, 2)
        a.start()
        self.copy(self.right, None, 3, 1).wait_recv()
        b = self.copy(self.right, 1, 3, 3)
        b.start()
        self.sent.extend([a, b])

    def finish(self):
        self.copy(self.far, 0, 1, 2).wait_recv()
        self.copy(self.far, 1, 3, 3).wait_recv()


def kernel(
    x_ref, gate_ref, b_ref, c_ref, ld_ref, gain_ref, w_ref, res_ref, kept_ref, got_ref,
    W, X, G, B, C, LD, RES, cum_s, cum_t, ecx, within, ent, thr, NB, ACT, away, keep, kin,
    sib_out, sib_in, row_out, row_in, col, back_out, back_in, inc_out, inc,
    load_sem, s0, r0, s1, r1, s2, r2, sx, rx, sa, ra, sf, rf, sr, rr, sk, rk, out_sem,
):
    pos = place()
    x, y, z, c = pos
    sibling = device(x, y, z, 1 - c)
    sent = []

    loads = []
    for i, (src, dst) in enumerate((
        (ld_ref, LD), (w_ref, W.at[x, y, 0]), (x_ref, X), (b_ref, B), (c_ref, C), (gate_ref, G), (res_ref, RES),
    )):
        loads.append(pltpu.make_async_copy(src, dst, load_sem.at[i]))
        loads[-1].start()

    barrier = pltpu.get_barrier_semaphore()
    even = 1 - lax.rem(z, 2)
    za, zb = around(z, 3 - 2 * even), around(z, 1 + 2 * even)
    zo = around(z, 2)
    partners = [sibling] + [shifted(pos, a, d) for a in range(2) for d in (1, 3, 2)]
    partners += [device(x, y, zz, cc) for zz in (za, zb) for cc in (0, 1)]
    for p in partners:
        pl.semaphore_signal(barrier, inc=1, device_id=p, device_id_type=MESH)

    def push(src, dst, send, recv, target):
        cp = pltpu.make_async_remote_copy(
            src_ref=src, dst_ref=dst, send_sem=send, recv_sem=recv, device_id=target, device_id_type=MESH
        )
        cp.start()
        sent.append(cp)

    def arrived(dst, send, recv):
        pltpu.make_async_remote_copy(
            src_ref=dst, dst_ref=dst, send_sem=send, recv_sem=recv, device_id=sibling, device_id_type=MESH
        ).wait_recv()

    def sems(array, *at):
        return lambda k: array.at[(*at, k)]

    ph1, ph2 = [], []
    for part in range(4):
        slot, first = part // 2, part % 2 * 512
        a1, a2 = (1, 0) if part % 2 == 0 else (0, 1)
        ph1.append(RingGather(W, pos, [x, y, slot], a1, first, sems(s1, part), sems(r1, part), sent))
        subs = []
        for j, d in enumerate((0, 3, 1, 2)):
            index = [x, y, slot]
            index[a1] = around(pos[a1], d)
            subs.append(RingGather(W, pos, index, a2, first, sems(s2, part, j), sems(r2, part, j), sent))
        ph2.append(subs)

    tri_r = lax.broadcasted_iota(jnp.int32, (SPAN, SPAN), 0)
    tri_c = lax.broadcasted_iota(jnp.int32, (SPAN, SPAN), 1)
    lower = tri_r >= tri_c
    tri = jnp.where(tri_r <= tri_c, 1.0, 0.0).astype(BF16)
    head_of = lax.div(lax.broadcasted_iota(jnp.int32, (2 * HEADS, FEATS), 1), HEAD_DIM)
    head_at = lax.rem(lax.broadcasted_iota(jnp.int32, (2 * HEADS, FEATS), 0), HEADS)
    spread = jnp.where(head_of == head_at, 1.0, 0.0).astype(BF16)

    def expand(v):
        hi = v.astype(BF16)
        lo = (v - hi.astype(F32)).astype(BF16)
        return dot(jnp.concatenate([hi, lo], axis=1), spread)

    loads[0].wait()
    for s in range(SPANS):
        hi, mid, lo = split3(LD[:, s * SPAN:(s + 1) * SPAN])
        cum = dot(hi, tri) + dot(mid, tri) + dot(lo, tri)
        cum_t[s] = cum
        cum_s[s] = cum.T
    ent[0] = jnp.zeros((STATE, FEATS), F32)
    thr[0] = jnp.ones((8, FEATS), F32)
    for i in (2, 3):
        loads[i].wait()

    def fresh(s):
        rows = slice(s * SPAN, (s + 1) * SPAN)
        cum = cum_s[s]
        weights = expand(jnp.exp(cum[SPAN - 1:, :] - cum))
        weighted = (X[rows, :].astype(F32) * weights).astype(BF16)
        new = dot(B[rows, :], weighted, ((0,), (0,)))
        ecx[s] = expand(jnp.exp(cum))
        decay = ecx[s, SPAN - 1:, :]
        ent[s + 1] = decay * ent[s] + new
        thr[s + 1] = thr[s] * decay

    for s in range(SPANS):
        fresh(s)

    loads[1].wait()
    pl.semaphore_wait(barrier, len(partners))
    odd_y = lax.rem(y, 2)

    def sharer(odd):
        return device(x, y, around(z, (1 - odd) * (3 - 2 * even) + odd * (1 + 2 * even)), c)

    push(W.at[x, y, 0], W.at[x, y, 1], s0, r0, sharer(odd_y))

    def half_block(k, slot):
        d = (3, 1, 2)[k % 3]
        bx, by = (x, around(y, d)) if k < 3 else (around(x, d), y)
        return W.at[bx, by, slot, pl.ds(k // 3 * 512, 512)], lax.rem(by, 2)

    def hand(k):
        src, odd = half_block(k, 0)
        push(src, half_block(k, 1)[0], s1.at[2 + k // 3, k % 3], r1.at[2 + k // 3, k % 3], sharer(odd))

    ph1[0].start()
    ph1[1].start()
    ph2[0][0].start()

    mine = pl.ds(pl.multiple_of(c * HALF, HALF), HALF)
    other = pl.ds(pl.multiple_of((1 - c) * HALF, HALF), HALF)

    def message(state, decay):
        hi = decay.astype(BF16)
        lo = (decay - hi.astype(F32)).astype(BF16)
        shape = (8, decay.shape[1])
        return state.astype(BF16), jnp.concatenate([jnp.broadcast_to(hi, shape), jnp.broadcast_to(lo, shape)], axis=0)

    def opened(block):
        return block[:STATE].astype(F32), block[STATE:STATE + 1].astype(F32) + block[STATE + 8:STATE + 9].astype(F32)

    sib_out[:STATE], sib_out[STATE:] = message(ent[SPANS, :, other], thr[SPANS, 0:1, other])
    push(sib_out, sib_in, sx.at[0], rx.at[0], sibling)

    for i in (4, 5):
        loads[i].wait()

    lane_low = lax.broadcasted_iota(jnp.int32, (128, 128), 1) < HEAD_DIM

    def within_span(s):
        rows = slice(s * SPAN, (s + 1) * SPAN)
        scores = dot(C[rows, :], B[rows, :], ((1,), (1,)))
        scores = jnp.where(lower, scores, 0.0)
        top, bottom = scores[:128, :128], scores[128:, :]
        cum, cum_row = cum_s[s], cum_t[s]
        g = G[rows, :].astype(F32)
        silu = g / (1.0 + jnp.exp(-g))
        ecx[s] = ecx[s] * silu
        for pair in range(HEADS // 2):
            lanes = slice(pair * 128, (pair + 1) * 128)
            xs = X[rows, lanes]
            tops, bottoms = [], []
            for h in (2 * pair, 2 * pair + 1):
                col, row = cum[:, h:h + 1], cum_row[h:h + 1, :]
                mix = (jnp.exp(jnp.minimum(col[:128] - row[:, :128], 0.0)) * top).astype(BF16)
                tops.append(dot(mix, xs[:128]))
                mix = (jnp.exp(jnp.minimum(col[128:] - row, 0.0)) * bottom).astype(BF16)
                bottoms.append(dot(mix, xs))
            within[s, :128, lanes] = jnp.where(lane_low, tops[0], tops[1]) * silu[:128, lanes]
            within[s, 128:, lanes] = jnp.where(lane_low, bottoms[0], bottoms[1]) * silu[128:, lanes]

    arrived(sib_in, sx.at[0], rx.at[0])
    first_core = c == 0
    own_state, own_decay = ent[SPANS, :, mine], thr[SPANS, 0:1, mine]
    sib_state, sib_decay = opened(sib_in[...])
    state0 = jnp.where(first_core, own_state, sib_state)
    state1 = jnp.where(first_core, sib_state, own_state)
    decay0 = jnp.where(first_core, own_decay, sib_decay)
    decay1 = jnp.where(first_core, sib_decay, own_decay)
    chip_state, chip_decay = message(decay1 * state0 + state1, decay0 * decay1)
    for t in range(4):
        row_out[t, :STATE] = chip_state[:, t * 128:(t + 1) * 128]
        row_out[t, STATE:] = chip_decay[:, t * 128:(t + 1) * 128]
    for i in (2, 1, 3):
        to = around(y, i)
        push(row_out.at[to], row_in.at[y], sx.at[i], rx.at[i], shifted(pos, 1, i))
    row_in[y] = row_out[y]
    ph1[1].forward()
    ph1[0].forward()
    for k in (3, 4, 0, 1):
        hand(k)

    within_span(0)

    for i in (1, 3, 2):
        arrived(row_in.at[around(y, 4 - i)], sx.at[i], rx.at[i])
    before_y, through_y = [jnp.zeros((STATE, 128), F32)], [jnp.ones((1, 128), F32)]
    for t in range(4):
        state, decay = opened(row_in[t])
        before_y.append(decay * before_y[t] + state)
        through_y.append(through_y[t] * decay)
    row_state, row_decay = message(before_y[4], through_y[4])
    col[x, :STATE] = row_state
    col[x, STATE:] = row_decay
    for i in (2, 1, 3):
        push(col.at[x], col.at[x], sx.at[3 + i], rx.at[3 + i], shifted(pos, 0, i))

    ph2[1][0].start()
    ph1[0].finish()
    ph2[0][1].start()
    ph1[1].finish()
    for k in (5, 2):
        hand(k)

    within_span(1)

    for i in (1, 3, 2):
        arrived(col.at[around(x, 4 - i)], sx.at[3 + i], rx.at[3 + i])
    before_x = jnp.zeros((STATE, 128), F32)
    for t in range(4):
        state, decay = opened(col[t])
        before_x = jnp.where(t < x, decay * before_x + state, before_x)
    for t in range(4):
        back_out[t] = (through_y[t] * before_x + before_y[t]).astype(BF16)
    for i in (2, 1, 3):
        to = around(y, i)
        push(back_out.at[to], back_in.at[y], sx.at[6 + i], rx.at[6 + i], shifted(pos, 1, i))
    back_in[y] = back_out[y]

    for j in (1, 2, 3):
        ph2[1][j].start()
        if j > 1:
            ph2[0][j].start()

    within_span(2)

    for i in (1, 3, 2):
        arrived(back_in.at[around(y, 4 - i)], sx.at[6 + i], rx.at[6 + i])
    enter0 = jnp.concatenate([back_in[t] for t in range(4)], axis=1).astype(F32)
    enter1 = decay0 * enter0 + state0
    inc[c] = jnp.where(first_core, enter0, enter1).astype(BF16)
    inc_out[...] = jnp.where(first_core, enter1, enter0).astype(BF16)
    push(inc_out, inc.at[c], sx.at[10], rx.at[10], sibling)

    ph2[0][0].forward()
    ph2[1][0].forward()

    within_span(3)

    arrived(W.at[x, y, 1], s0, r0)
    for k in range(6):
        arrived(half_block(k, 1)[0], s1.at[2 + k // 3, k % 3], r1.at[2 + k // 3, k % 3])
    for j in range(4):
        ph2[2][j].start()
        ph2[3][j].start()

    arrived(inc.at[1 - c], sx.at[10], rx.at[10])

    def normed(q, first=0, count=SPAN):
        rows = pl.ds(pl.multiple_of(q * SPAN + first, 128), count)
        incoming = jnp.concatenate([inc[0], inc[1]], axis=1).astype(F32)
        state = (ent[q] + thr[q, 0:1, :] * incoming).astype(BF16)
        here = slice(first, first + count)
        gated = within[q, here] + dot(C[rows, :], state) * ecx[q, here]
        factor = lax.rsqrt(jnp.mean(gated * gated, axis=1, keepdims=True) + 1e-05)
        return (gated * factor * gain_ref[...]).astype(BF16)

    for h in (0, 1):
        half = slice(h * 128, (h + 1) * 128)
        NB[half] = normed(zo, h * 128, 128)
        push(NB.at[half], ACT.at[3, c, half], sa.at[4 * h], ra.at[4 * h], device(x, y, za, c))
        push(NB.at[half], ACT.at[4, c, half], sa.at[4 * h + 1], ra.at[4 * h + 1], device(x, y, zb, c))
    ACT[1, c] = normed(za)
    push(ACT.at[1, c], ACT.at[5, c], sa.at[2], ra.at[2], device(x, y, za, c))
    ACT[2, c] = normed(zb)
    push(ACT.at[2, c], ACT.at[6, c], sa.at[3], ra.at[3], device(x, y, zb, c))

    def share(slot):
        push(ACT.at[slot, c], ACT.at[slot, c], sf.at[slot], rf.at[slot], sibling)

    share(1)
    share(2)
    ACT[0, c] = normed(z)
    share(0)

    for j in (1, 2, 3):
        ph2[0][j].forward()
        ph2[1][j].forward()

    for i in (0, 1):
        for h in (0, 1):
            arrived(ACT.at[3 + i, c, h * 128:(h + 1) * 128], sa.at[4 * h + i], ra.at[4 * h + i])
        share(3 + i)
    for j in range(4):
        ph2[2][j].forward()
        ph2[3][j].forward()
    for slot in (1, 2, 3, 4):
        arrived(ACT.at[slot, 1 - c], sf.at[slot], rf.at[slot])

    def product(own, other, b0, b1):
        lhs = jnp.concatenate([ACT[own].reshape(2 * SPAN, FEATS), ACT[other].reshape(2 * SPAN, FEATS)], axis=1)
        rhs = jnp.concatenate([W[b[0], b[1]].reshape(2 * FEATS, 128) for b in (b0, b1)], axis=1)
        return dot(lhs, rhs)

    def columns(bx, by, core):
        return pl.ds(pl.multiple_of((bx * 8 + by * 2 + core) * 128, 128), 128)

    def away_copy(bx, by, section):
        odd = lax.rem(by, 2)
        target = around(z, (1 - odd) * (1 + 2 * even) + odd * (3 - 2 * even))
        return pltpu.make_async_remote_copy(
            src_ref=away.at[bx, by, section], dst_ref=got_ref.at[:, columns(bx, by, c)],
            send_sem=sr.at[bx, by, section], recv_sem=rr.at[bx, by, c],
            device_id=device(x, y, target, section), device_id_type=MESH,
        )

    def keep_remote(bx, by):
        return pltpu.make_async_remote_copy(
            src_ref=keep.at[bx, by], dst_ref=kin.at[bx, by],
            send_sem=sk.at[bx, by], recv_sem=rk.at[bx, by], device_id=sibling, device_id_type=MESH,
        )

    near = (((0, 3), (0, 1)), ((3, 3), (3, 1)), ((1, 3), (1, 1)), ((0, 0), (3, 0)))
    rest = (((1, 0), (2, 0)), ((2, 3), (2, 1)), ((0, 2), (1, 2)), ((2, 2), (3, 2)))

    def over_pairs(table, body):
        @pl.loop(0, 4)
        def _(i):
            def pick(b, axis):
                value = table[0][b][axis]
                for k in (1, 2, 3):
                    value = jnp.where(i == k, table[k][b][axis], value)
                return around(pos[axis], value)

            body((pick(0, 0), pick(0, 1)), (pick(1, 0), pick(1, 1)))

    def send_away(b0, b1):
        odd = lax.rem(b0[1], 2)
        result = product(2 - odd, 3 + odd, b0, b1)
        for k, (bx, by) in enumerate((b0, b1)):
            for section in (0, 1):
                away[bx, by, section] = result[section * SPAN:(section + 1) * SPAN, k * 128:(k + 1) * 128].astype(BF16)
                away_copy(bx, by, section).start()

    def keep_here(b0, b1):
        odd = lax.rem(b0[1], 2)
        result = product(0, 5 + odd, b0, b1)
        for k, (bx, by) in enumerate((b0, b1)):
            parts = [result[section * SPAN:(section + 1) * SPAN, k * 128:(k + 1) * 128] for section in (0, 1)]
            keep[bx, by] = jnp.where(first_core, parts[1], parts[0]).astype(BF16)
            keep_remote(bx, by).start()
            lanes = columns(bx, by, c)
            RES[:, lanes] = (RES[:, lanes].astype(F32) + jnp.where(first_core, parts[0], parts[1])).astype(BF16)

    over_pairs(near, send_away)
    for i in (2, 3):
        arrived(ACT.at[3 + i, c], sa.at[i], ra.at[i])
        share(3 + i)
    for t in ph2:
        for j in range(4):
            t[j].finish()
    over_pairs(rest, send_away)
    for slot in (0, 5, 6):
        arrived(ACT.at[slot, 1 - c], sf.at[slot], rf.at[slot])
    loads[6].wait()
    over_pairs(near, keep_here)
    over_pairs(rest, keep_here)

    @pl.loop(0, 16)
    def _(i):
        bx, by = lax.div(i, 4), lax.rem(i, 4)
        keep_remote(bx, by).wait_send()
        arrived(kin.at[bx, by], sk.at[bx, by], rk.at[bx, by])
        lanes = columns(bx, by, 1 - c)
        RES[:, lanes] = (RES[:, lanes].astype(F32) + kin[bx, by].astype(F32)).astype(BF16)

    kept_copy = pltpu.make_async_copy(RES, kept_ref, out_sem)
    kept_copy.start()

    for cp in sent:
        cp.wait_send()
    kept_copy.wait()

    @pl.loop(0, 16)
    def _(i):
        bx, by = lax.div(i, 4), lax.rem(i, 4)
        for section in (0, 1):
            away_copy(bx, by, section).wait_send()
        for core in (0, 1):
            arrived(got_ref.at[:, columns(bx, by, core)], sr.at[bx, by, core], rr.at[bx, by, core])


def per_device(
    head_inputs, gate_input, state_write, state_read, log_decay, norm_gain, out_weight, residual
):
    any_space = pl.BlockSpec(memory_space=pl.ANY)
    vmem, dma = pltpu.VMEM, pltpu.SemaphoreType.DMA
    kept, got = pl.pallas_call(
        kernel,
        out_shape=[jax.ShapeDtypeStruct(residual.shape, BF16)] * 2,
        in_specs=[any_space] * 5 + [pl.BlockSpec(memory_space=pltpu.VMEM)] + [any_space] * 2,
        out_specs=[any_space] * 2,
        scratch_shapes=[
            vmem((4, 4, 2, 1024, 128), BF16),
            vmem((TOKENS, FEATS), BF16),
            vmem((TOKENS, FEATS), BF16),
            vmem((TOKENS, STATE), BF16),
            vmem((TOKENS, STATE), BF16),
            vmem((HEADS, TOKENS), F32),
            vmem((SPAN, 4096), BF16),
                vmem((SPANS, SPAN, HEADS), F32),
            vmem((SPANS, HEADS, SPAN), F32),
            vmem((SPANS, SPAN, FEATS), F32),
            vmem((SPANS, SPAN, FEATS), F32),
            vmem((SPANS + 1, STATE, FEATS), F32),
            vmem((SPANS + 1, 8, FEATS), F32),
            vmem((SPAN, FEATS), BF16),
            vmem((7, 2, SPAN, FEATS), BF16),
            vmem((4, 4, 2, SPAN, 128), BF16),
            vmem((4, 4, SPAN, 128), BF16),
            vmem((4, 4, SPAN, 128), BF16),
            vmem((MESSAGE, HALF), BF16),
            vmem((MESSAGE, HALF), BF16),
            vmem((4, MESSAGE, 128), BF16),
            vmem((4, MESSAGE, 128), BF16),
            vmem((4, MESSAGE, 128), BF16),
            vmem((4, STATE, 128), BF16),
            vmem((4, STATE, 128), BF16),
            vmem((STATE, HALF), BF16),
            vmem((2, STATE, HALF), BF16),
            dma((7,)),
            dma, dma, dma((4, 4)), dma((4, 4)), dma((4, 4, 4)), dma((4, 4, 4)),
            dma((11,)), dma((11,)),
            dma((6,)), dma((6,)),
            dma((7,)), dma((7,)),
            dma((4, 4, 2)), dma((4, 4, 2)),
            dma((4, 4)), dma((4, 4)), dma,
        ],
        compiler_params=pltpu.CompilerParams(
            collective_id=0, has_side_effects=True, vmem_limit_bytes=60 << 20
        ),
        cost_estimate=pl.CostEstimate(flops=11 * 10**9, bytes_accessed=12 << 20, transcendentals=4 << 20),
        name="spanned_mixer",
    )(head_inputs, gate_input, state_write, state_read, log_decay.T, norm_gain.reshape(1, -1), out_weight, residual)
    return (kept.astype(F32) + got.astype(F32)).astype(BF16)


def solution(mesh):
    placed = (
        P("ctx", ("segment", "mp")),
        P("ctx", ("segment", "mp")),
        P("ctx", ("segment", "mp")),
        P("ctx", ("segment", "mp")),
        P("ctx", ("segment", "mp")),
        P(("segment", "mp")),
        P(("segment", "mp"), "ctx"),
        P(("ctx", "segment", "mp"), None),
    )
    return jax.shard_map(
        per_device,
        mesh=mesh,
        in_specs=placed,
        out_specs=P(("ctx", "segment", "mp"), None),
        check_vma=False,
    )
```
